256 devices in a mesh: row: 8 (over y, x_hi), col: 32 (over z, x_lo, core).
Axes of the slice: x: 4 (x_hi: 2, x_lo: 2; x = x_hi * 2 + x_lo), y: 4, z: 8, core: 2. Of those that a mesh axis runs over, the one named last changes fastest.
Arguments:
- query_proj: bfloat16 [128, 1536, 128], P('row', 'col'), may hold values from -6 to 6
- key_proj: bfloat16 [128, 1536, 128], P('row', 'col'), may hold values from -6 to 6
- value_proj: bfloat16 [128, 1536, 128], P('row', 'col'), may hold values from -6 to 6
- attn_out: bfloat16 [128, 1536, 128], P('row', 'col'), may hold values from -6 to 6
- out_grad: bfloat16 [128, 1536, 128], P('row', 'col'), may hold values from -6 to 6
- log_norm: float32 [4, 128, 1536], P(None, 'row', 'col'), may hold values from 3 to 5
- pair_mask: int32 [128, 1536], P('row'), may hold values 0 or 1
- pair_bias: bfloat16 [4, 1536, 1536], P(None, 'col', 'row'), may hold values from -6 to 6
Outputs:
- query_grad: bfloat16 [128, 1536, 128], P('row', 'col')
- key_grad: bfloat16 [128, 1536, 128], P('row', 'col')
- value_grad: bfloat16 [128, 1536, 128], P('row', 'col')
- bias_grad: bfloat16 [4, 1536, 1536], P(None, 'col', 'row')
The draws below stay inside these ranges and needn't reach their ends.
All inputs are finite; a program needn't handle non-finite values. No bound on the sum of `pair_mask` on one device may be relied on, other than what follows from the above.
Results may differ from the reference program's by a relative error of at most 0.0051.
Values may be sent and summed in bfloat16 or wider, within the bound.
A program may use at most 192 MiB of HBM per device.

```python
import jax
import jax.numpy as jnp
from jax import lax

HEADS = 4
HEAD_DIM = 32
FEATURES = 128
N_TOK = 1536
ROWS = 128


def set_ends(drawn, rng, low, high):
    extent = drawn.shape
    index_at = [jax.random.randint(jax.random.fold_in(rng, axis), (), 0, extent[axis]) for axis in range(len(extent))]
    drawn = drawn.at[tuple(index_at)].set(low)
    longest = extent.index(max(extent))
    index_at[longest] = (index_at[longest] + 1) % extent[longest]
    return drawn.at[tuple(index_at)].set(high)


def level_of(stream_key, extent, shards, smallest, largest):
    factor_of = 1.0
    for axis_at, shards_of in shards:
        draws = jax.random.uniform(jax.random.fold_in(jax.random.fold_in(stream_key, 6), axis_at), (shards_of,), jnp.float32, smallest / len(shards), largest / len(shards))
        factor_of = factor_of * jnp.repeat(jnp.exp(draws), extent[axis_at] // shards_of).reshape((-1,) + (1,) * (len(extent) - 1 - axis_at))
    return factor_of


def centred(key, dims, width, bound, pieces=(), dtype=jnp.bfloat16):
    entries = jax.random.normal(key, dims, jnp.float32) * width
    if len(pieces) > 0:
        entries = level_of(key, dims, pieces, -0.22, 0.18) * entries
    return jnp.clip(entries, min=-bound, max=bound).astype(dtype)


def setup_inputs(seed: int = 0) -> dict:
    streams_of = jax.random.split(jax.random.key(seed), 9)
    return {
        "query_proj": centred(streams_of[0], (ROWS, N_TOK, FEATURES), 1.0, 6.0, ((0, 8), (1, 32))),
        "key_proj": centred(streams_of[1], (ROWS, N_TOK, FEATURES), 1.0, 6.0, ((0, 8), (1, 32))),
        "value_proj": centred(streams_of[2], (ROWS, N_TOK, FEATURES), 1.0, 6.0, ((0, 8), (1, 32))),
        "attn_out": centred(streams_of[3], (ROWS, N_TOK, FEATURES), 1.0, 6.0, ((0, 8), (1, 32))),
        "out_grad": centred(streams_of[4], (ROWS, N_TOK, FEATURES), 1.0, 6.0, ((0, 8), (1, 32))),
        "log_norm": jnp.clip(3.0 + 2.0 * jax.random.uniform(streams_of[5], (HEADS, ROWS, N_TOK), jnp.float32) ** level_of(streams_of[5], (HEADS, ROWS, N_TOK), ((1, 8), (2, 32)), -0.2, 0.2), 3.0, 5.0),
        "pair_mask": set_ends((jax.random.randint(streams_of[6], (ROWS, N_TOK), 0, 8) < 7).astype(jnp.int32), jax.random.fold_in(streams_of[6], 1), 0, 1),
        "pair_bias": centred(streams_of[7], (HEADS, N_TOK, N_TOK), 1.0, 6.0, ((1, 32), (2, 8))),
    }


def reference(query_proj, key_proj, value_proj, attn_out, out_grad, log_norm, pair_mask, pair_bias):
    scaling = HEAD_DIM ** -0.5
    bias_full = pair_bias.astype(jnp.float32)

    def to_heads(block):
        return block.astype(jnp.float32).reshape(N_TOK, HEADS, HEAD_DIM)

    def one_row(bias_total, row_inputs):
        query_row, key_row, value_row, out_row, grad_row, norm_row, mask_row = row_inputs
        queries = to_heads(query_row)
        keys_row = to_heads(key_row)
        values_row = to_heads(value_row)
        outputs = to_heads(out_row)
        grads = to_heads(grad_row)
        scores = jnp.einsum('jhd,khd->hjk', queries, keys_row) * scaling + bias_full
        attention = jnp.where(mask_row[None, None, :] == 1, jnp.exp(scores - norm_row[:, :, None]), 0.0)
        probs_low = lax.optimization_barrier(attention.astype(jnp.bfloat16)).astype(jnp.float32)
        delta_row = jnp.sum(grads * outputs, axis=2).T
        prob_grad = jnp.einsum('jhd,khd->hjk', grads, values_row)
        score_grad = attention * (prob_grad - delta_row[:, :, None])
        score_low = lax.optimization_barrier(score_grad.astype(jnp.bfloat16)).astype(jnp.float32)
        grad_query = jnp.einsum('hjk,khd->jhd', score_low, keys_row) * scaling
        grad_key = jnp.einsum('hjk,jhd->khd', score_low, queries) * scaling
        grad_value = jnp.einsum('hjk,jhd->khd', probs_low, grads)
        outs_row = (grad_query.reshape(N_TOK, FEATURES).astype(jnp.bfloat16),
                    grad_key.reshape(N_TOK, FEATURES).astype(jnp.bfloat16),
                    grad_value.reshape(N_TOK, FEATURES).astype(jnp.bfloat16))
        return bias_total + score_grad, outs_row

    initial = jnp.zeros((HEADS, N_TOK, N_TOK), jnp.float32)
    norms = jnp.transpose(log_norm, (1, 0, 2))
    bias_total, grads_all = lax.scan(one_row, initial, (query_proj, key_proj, value_proj, attn_out, out_grad, norms, pair_mask))
    return grads_all[0], grads_all[1], grads_all[2], bias_total.astype(jnp.bfloat16)
```

```python
import functools

import jax
import jax.numpy as jnp
from jax import lax
from jax.experimental import pallas as pl
from jax.experimental.pallas import tpu as pltpu
from jax.sharding import PartitionSpec as P

MESH = pl.DeviceIdType.MESH
HEADS = 4
BIG = 1.0e30
F32 = jnp.float32
BF16 = jnp.bfloat16
NT = (((1,), (1,)), ((), ()))
TN = (((0,), (0,)), ((), ()))


def iota(shape, axis):
    return lax.broadcasted_iota(jnp.int32, shape, axis)


def split3(value):
    high = value.astype(BF16).astype(F32)
    rest = value - high
    middle = rest.astype(BF16).astype(F32)
    low = (rest - middle).astype(BF16).astype(F32)
    return high, middle, low


def kernel(
    geometry, scaling,
    q_ref, k_ref, v_ref, o_ref, g_ref, ln_ref, madd_ref, bias_ref,
    dq_out, dk_out, dv_out, db_out,
    qg, st, st_out, kx, vx, ws, wp, bias_all,
    acc_in, acc_out, dq_own, dk_acc, dv_acc, db_acc,
    back, db_send, db_core, db_keep, db_y, db_ysum, db_x, db_home,
    x_send, x_recv, x_local, r_send, r_recv, s_send, s_recv, a_send, a_recv,
    b_send, b_recv, d_send, d_recv, e_send, e_recv, e_local, h_local,
):
    ny, nxh, nz = geometry
    nx = 2 * nxh
    row = lax.axis_index("row")
    col = lax.axis_index("col")
    y, xh = lax.div(row, nxh), lax.rem(row, nxh)
    z, quad = lax.div(col, 4), lax.rem(col, 4)
    xl, core = lax.div(quad, 2), lax.rem(quad, 2)
    x = xh * 2 + xl
    right, left = lax.rem(z + 1, nz), lax.rem(z + nz - 1, nz)
    right_id = {"col": right * 4 + quad}
    left_id = {"col": left * 4 + quad}
    quad_ids = [{"col": z * 4 + lax.rem(quad + o, 4)} for o in range(1, 4)]
    quad_of = [lax.rem(quad + o, 4) for o in range(1, 4)]
    xs = [lax.rem(x + o, nx) for o in range(1, nx)]
    x_ids = [
        {"row": y * nxh + lax.div(p, 2), "col": z * 4 + lax.rem(p, 2) * 2 + core} for p in xs
    ]
    ys = [lax.rem(y + o, ny) for o in range(1, ny)]
    y_ids = [{"row": p * nxh + xh} for p in ys]
    core_id = {"col": z * 4 + xl * 2 + 1 - core}
    first = xl == 0
    source_step = jnp.where(first, lax.rem(row - z + nz, nz), lax.rem(z - row + nz, nz))
    to_plane = {"row": source_step, "col": row * 4 + quad}
    home_z = jnp.where(first, lax.rem(z - row + nz, nz), lax.rem(z + row, nz))
    to_home = {"row": z, "col": home_z * 4 + quad}
    alone = jnp.logical_and(row == 0, z == 0)

    barrier = pltpu.get_barrier_semaphore()
    greeted = quad_ids + [right_id, left_id] + x_ids + y_ids
    for peer in greeted:
        pl.semaphore_signal(barrier, inc=1, device_id=peer, device_id_type=MESH)

    @pl.when(jnp.logical_not(alone))
    def _():
        pl.semaphore_signal(barrier, inc=1, device_id=to_plane, device_id_type=MESH)
        pl.semaphore_signal(barrier, inc=1, device_id=to_home, device_id_type=MESH)

    pl.semaphore_wait(barrier, len(greeted) + jnp.where(alone, 0, 2))

    def remote(source, target, send, recv, device):
        return pltpu.make_async_remote_copy(
            src_ref=source, dst_ref=target, send_sem=send, recv_sem=recv,
            device_id=device, device_id_type=MESH,
        )

    bias_mine = bias_all.at[row, core, xl]
    bias_push = remote(
        bias_ref, bias_all.at[source_step, core, xl], b_send.at[0], b_recv.at[0], to_plane
    )
    bias_self = pltpu.make_async_copy(bias_ref, bias_mine, h_local.at[0])

    @pl.when(jnp.logical_not(alone))
    def _():
        bias_push.start()

    @pl.when(alone)
    def _():
        bias_self.start()

    half, place = xl, pl.ds(pl.multiple_of(core * 48, 48), 48)
    mine = pl.ds(pl.multiple_of(quad * 48, 48), 48)
    pairs = [
        (q_ref, qg.at[0, :, half, 0, place, :]),
        (g_ref, qg.at[0, :, half, 1, place, :]),
        (k_ref, kx.at[:, mine, :]),
        (v_ref, vx.at[:, mine, :]),
    ]
    swaps = []
    for at, (source, target) in enumerate(pairs):
        for o in range(3):
            copy = remote(
                source.at[pl.ds(4 * quad_of[o], 4)], target,
                x_send.at[at, o], x_recv.at[at, o], quad_ids[o],
            )
            copy.start()
            swaps.append(copy)
        copy = pltpu.make_async_copy(source.at[pl.ds(4 * quad, 4)], target, x_local.at[at])
        copy.start()
        swaps.append(copy)

    lane = iota((48, 128), 1)
    term = lax.rem(lane, 8)
    norm = ln_ref[...] * F32(scaling ** -1)
    norm_terms = [part.astype(BF16) for part in split3(norm)]
    source_lane, target_lane = iota((128, 128), 0), iota((128, 128), 1)
    target_term = lax.rem(target_lane, 8)
    same_head = lax.div(source_lane, 32) == lax.rem(lax.div(target_lane, 8), 4)
    delta_term = jnp.logical_and(target_term >= 3, target_term < 6)
    norm_source, norm_target = iota((64, 128), 0), iota((64, 128), 1)
    norm_term = lax.rem(norm_target, 8) < 3

    def stats(target, carry):
        total = jnp.zeros((48, 128), F32)
        pick = jnp.where(
            jnp.logical_and(norm_source - target * 16 == lax.div(norm_target, 8), norm_term), 1.0, 0.0
        ).astype(BF16)
        for part in norm_terms:
            total += jnp.dot(part, pick, preferred_element_type=F32)
        for i in range(4):
            gather = jnp.where(
                jnp.logical_and(
                    jnp.logical_and(same_head, delta_term), lax.div(target_lane, 32) == i
                ), 1.0, 0.0,
            ).astype(BF16)
            product = g_ref[target * 4 + i].astype(F32) * o_ref[target * 4 + i].astype(F32)
            high = product.astype(BF16)
            low = (product - high.astype(F32)).astype(BF16)
            total += jnp.dot(high, gather, preferred_element_type=F32)
            total += jnp.dot(low, gather, preferred_element_type=F32)
        high, middle, low = split3(-total)
        value = jnp.where(
            jnp.logical_or(term == 0, term == 3), high,
            jnp.where(jnp.logical_or(term == 1, term == 4), middle,
                      jnp.where(jnp.logical_or(term == 2, term == 5), low,
                                jnp.where(term == 6, 1.0, 0.0))),
        )
        st_out[target] = value.astype(BF16)
        return carry

    lax.fori_loop(0, 4, stats, 0)
    target = st.at[0, half, place, :]
    for o in range(3):
        copy = remote(st_out.at[quad_of[o]], target, x_send.at[4, o], x_recv.at[4, o], quad_ids[o])
        copy.start()
        swaps.append(copy)
    copy = pltpu.make_async_copy(st_out.at[quad], target, x_local.at[4])
    copy.start()
    swaps.append(copy)

    @pl.when(jnp.logical_not(alone))
    def _():
        bias_push.wait()

    @pl.when(alone)
    def _():
        bias_self.wait()

    bias_copies = []
    for o in range(nx - 1):
        copy = remote(bias_mine, bias_mine, b_send.at[1 + o], b_recv.at[1 + o], x_ids[o])
        copy.start()
        bias_copies.append(copy)
    for copy in swaps:
        copy.wait()

    def pass_on(s, i):
        return [
            remote(qg.at[s, i, 0], qg.at[s + 1, i, 0], r_send.at[s, i, 0], r_recv.at[s + 1, i, 0], right_id),
            remote(qg.at[s, i, 1], qg.at[s + 1, i, 1], r_send.at[s, i, 1], r_recv.at[s + 1, i, 1], left_id),
        ]

    def pass_stats(s):
        return [
            remote(st.at[s, 0], st.at[s + 1, 0], s_send.at[s, 0], s_recv.at[s + 1, 0], right_id),
            remote(st.at[s, 1], st.at[s + 1, 1], s_send.at[s, 1], s_recv.at[s + 1, 1], left_id),
        ]

    for copy in pass_stats(0):
        copy.start()
    for i in range(4):
        for copy in pass_on(0, i):
            copy.start()
    for copy in bias_copies:
        copy.wait()

    column = bias_all.at[pl.ds(y * nxh, nxh), core]
    bias_copies = []
    for o in range(ny - 1):
        copy = remote(column, column, b_send.at[8 + o], b_recv.at[8 + o], y_ids[o])
        copy.start()
        bias_copies.append(copy)

    wide_lane = iota((192, 128), 1)

    def weights(i, carry):
        keys, values, masked = kx[i], vx[i], madd_ref[i]
        for h in range(HEADS):
            head = lax.div(wide_lane, 32) == h
            block = pl.ds(h * 192, 192)
            first_lane = i * 32 + h * 8
            offset = wide_lane - first_lane
            zero = jnp.zeros((192, 128), F32)
            ws[i, block, 0:128] = jnp.where(head, keys.astype(F32), zero).astype(BF16)
            wp[i, block, 0:128] = jnp.where(head, values.astype(F32), zero).astype(BF16)
            ws[i, block, 128:256] = jnp.where(
                jnp.logical_and(offset >= 0, offset < 3), 1.0,
                jnp.where(offset == 6, masked.astype(F32), zero),
            ).astype(BF16)
            wp[i, block, 128:256] = jnp.where(
                jnp.logical_and(offset >= 3, offset < 6), 1.0, zero
            ).astype(BF16)
        dk_acc[i] = jnp.zeros(dk_acc.shape[1:], F32)
        dv_acc[i] = jnp.zeros(dv_acc.shape[1:], F32)
        return carry

    lax.fori_loop(0, 4, weights, 0)

    for copy in bias_copies:
        copy.wait()
    copy = remote(bias_all.at[:, core], bias_all.at[:, core], b_send.at[16], b_recv.at[16], core_id)
    copy.start()
    copy.wait()

    def one_row(s, i):
        @pl.when(s > 0)
        def _():
            before = pass_on(s - 1, i)
            for copy in before:
                copy.wait_recv()

            @pl.when(s < nz - 1)
            def _():
                for copy in pass_on(s, i):
                    copy.start()

        queries = jnp.concatenate([qg[s, i, 0, 0], qg[s, i, 1, 0]], axis=0)
        grads = jnp.concatenate([qg[s, i, 0, 1], qg[s, i, 1, 1]], axis=0)
        terms = jnp.concatenate([st[s, 0], st[s, 1]], axis=0)
        left_s = jnp.concatenate([queries, terms], axis=1)
        left_p = jnp.concatenate([grads, terms], axis=1)
        queries_t, grads_t = queries.T, grads.T
        grad_query = jnp.zeros((192, 128), F32)
        for t in range(3):
            span = pl.ds(256 * t, 256)
            logits = lax.dot_general(left_s, ws[i, span, :], NT, preferred_element_type=F32)
            prob_grad = lax.dot_general(left_p, wp[i, span, :], NT, preferred_element_type=F32)
            bias = jnp.concatenate(
                [bias_all[s, c, w, :, span] for w in range(2) for c in range(2)], axis=0
            ).astype(F32)
            probs = jnp.exp(logits * F32(scaling) + bias)
            score_grad = probs * prob_grad
            probs_low = probs.astype(BF16)
            score_low = score_grad.astype(BF16)

            @pl.when(i == 0)
            def _():
                db_acc[s, :, span] = score_grad

            @pl.when(i > 0)
            def _():
                db_acc[s, :, span] += score_grad

            grad_query += jnp.dot(score_low, ws[i, span, 0:128], preferred_element_type=F32)
            part = slice(32 * t, 32 * t + 64)
            dk_acc[i, t] += jnp.dot(queries_t[part], score_low, preferred_element_type=F32)
            dv_acc[i, t] += jnp.dot(grads_t[part], probs_low, preferred_element_type=F32)

        @pl.when(s == 0)
        def _():
            dq_own[i] = grad_query

        @pl.when(s == 1)
        def _():
            acc_out[1, i, 0] = grad_query[:96].astype(BF16)
            acc_out[1, i, 1] = grad_query[96:].astype(BF16)

        @pl.when(s > 1)
        def _():
            for copy in pass_sum(s - 1, i):
                copy.wait_recv()
            acc_out[s, i, 0] = (grad_query[:96] + acc_in[s, i, 0].astype(F32)).astype(BF16)
            acc_out[s, i, 1] = (grad_query[96:] + acc_in[s, i, 1].astype(F32)).astype(BF16)

        @pl.when(s > 0)
        def _():
            for copy in pass_sum(s, i):
                copy.start()

    def pass_sum(s, i):
        return [
            remote(acc_out.at[s, i, 0], acc_in.at[s + 1, i, 0], a_send.at[s, i, 0], a_recv.at[s + 1, i, 0], right_id),
            remote(acc_out.at[s, i, 1], acc_in.at[s + 1, i, 1], a_send.at[s, i, 1], a_recv.at[s + 1, i, 1], left_id),
        ]

    def one_step(s, carry):
        @pl.when(s > 0)
        def _():
            for copy in pass_stats(s - 1):
                copy.wait_recv()

            @pl.when(s < nz - 1)
            def _():
                for copy in pass_stats(s):
                    copy.start()

        def rows(i, inner):
            one_row(s, i)
            return inner

        return lax.fori_loop(0, 4, rows, carry)

    lax.fori_loop(0, nz, one_step, 0)

    def low(s, carry):
        for c in range(2):
            for w in range(2):
                start = (w * 2 + c) * 48
                db_send[s, c, w] = db_acc[s, start:start + 48, :].astype(BF16)
        return carry

    lax.fori_loop(0, nz, low, 0)
    core_copy = remote(db_send.at[:, 1 - core], db_core, d_send.at[0], d_recv.at[0], core_id)
    core_copy.start()

    result_lane = iota((192, 128), 1)

    def turned(acc, i, factor):
        blocks = []
        for t in range(3):
            unit = jnp.where(iota((64, 128), 0) + 32 * t == iota((64, 128), 1), 1.0, 0.0).astype(BF16)
            part = (acc[i, t] * F32(factor)).astype(BF16)
            blocks.append(lax.dot_general(part, unit, TN, preferred_element_type=F32))
        stacked = jnp.concatenate(blocks, axis=0)
        total = jnp.zeros((192, 128), F32)
        for h in range(HEADS):
            total = jnp.where(lax.div(result_lane, 32) == h, stacked[192 * h:192 * h + 192], total)
        return total.astype(BF16)

    def finish(i, carry):
        back[1, i] = turned(dk_acc, i, scaling)
        back[2, i] = turned(dv_acc, i, 1.0)
        return carry

    lax.fori_loop(0, 4, finish, 0)
    returns = []
    outs = (dq_out, dk_out, dv_out)

    def give_back(at):
        for o in range(3):
            columns = pl.ds(pl.multiple_of(quad_of[o] * 48, 48), 48)
            copy = remote(
                back.at[at, :, columns, :], outs[at].at[pl.ds(4 * quad, 4)],
                e_send.at[at, o], e_recv.at[at, o], quad_ids[o],
            )
            copy.start()
            returns.append(copy)
        copy = pltpu.make_async_copy(back.at[at, :, mine, :], outs[at].at[pl.ds(4 * quad, 4)], e_local.at[at])
        copy.start()
        returns.append(copy)

    give_back(1)
    give_back(2)

    def finish_query(i, carry):
        for copy in pass_sum(nz - 1, i):
            copy.wait_recv()
        for w in range(2):
            part = pl.ds(96 * w, 96)
            whole = dq_own[i, part, :] + acc_in[nz, i, w].astype(F32)
            back[0, i, part, :] = (whole * F32(scaling)).astype(BF16)
        return carry

    lax.fori_loop(0, 4, finish_query, 0)
    give_back(0)

    core_copy.wait()

    def over_cores(s, carry):
        for w in range(2):
            rows = pl.ds(pl.multiple_of(w * 96 + core * 48, 48), 48)
            whole = db_acc[s, rows, :] + db_core[s, w].astype(F32)
            db_acc[s, rows, :] = whole
            db_keep[s, w] = whole.astype(BF16)
        return carry

    lax.fori_loop(0, nz, over_cores, 0)
    copies = []
    for o in range(ny - 1):
        copy = remote(
            db_keep.at[pl.ds(ys[o] * nxh, nxh)], db_y.at[o], d_send.at[1 + o], d_recv.at[1 + o], y_ids[o]
        )
        copy.start()
        copies.append(copy)
    for copy in copies:
        copy.wait()
    for a in range(nxh):
        for w in range(2):
            rows = pl.ds(pl.multiple_of(w * 96 + core * 48, 48), 48)
            whole = db_acc[y * nxh + a, rows, :]
            for o in range(ny - 1):
                whole = whole + db_y[o, a, w].astype(F32)
            db_acc[y * nxh + a, rows, :] = whole
            db_ysum[a, w] = whole.astype(BF16)
    copies = []
    for o in range(nx - 1):
        copy = remote(
            db_ysum.at[lax.div(xs[o], 2), lax.rem(xs[o], 2)], db_x.at[o],
            d_send.at[8 + o], d_recv.at[8 + o], x_ids[o],
        )
        copy.start()
        copies.append(copy)
    for copy in copies:
        copy.wait()
    whole = db_acc[row, pl.ds(pl.multiple_of(xl * 96 + core * 48, 48), 48), :]
    for o in range(nx - 1):
        whole = whole + db_x[o].astype(F32)
    db_home[...] = whole.astype(BF16)
    home_push = remote(db_home, db_out, d_send.at[16], d_recv.at[16], to_home)
    home_self = pltpu.make_async_copy(db_home, db_out, h_local.at[1])

    @pl.when(jnp.logical_not(alone))
    def _():
        home_push.start()

    @pl.when(alone)
    def _():
        home_self.start()

    def sent(s, carry):
        def rows(i, inner):
            @pl.when(s < nz - 1)
            def _():
                for copy in pass_on(s, i):
                    copy.wait_send()

            @pl.when(s > 0)
            def _():
                for copy in pass_sum(s, i):
                    copy.wait_send()

            return inner

        lax.fori_loop(0, 4, rows, 0)

        @pl.when(s < nz - 1)
        def _():
            for copy in pass_stats(s):
                copy.wait_send()

        return carry

    lax.fori_loop(0, nz, sent, 0)
    for copy in returns:
        copy.wait()

    @pl.when(jnp.logical_not(alone))
    def _():
        home_push.wait()

    @pl.when(alone)
    def _():
        home_self.wait()


def solution(mesh):
    rows_n, cols_n = mesh.shape["row"], mesh.shape["col"]
    nz = cols_n // 4
    nxh = 2 if rows_n >= 4 else 1
    ny = rows_n // nxh
    nx = 2 * nxh

    def shards(query_proj, key_proj, value_proj, attn_out, out_grad, log_norm, pair_mask, pair_bias):
        width = query_proj.shape[2]
        scaling = (width // HEADS) ** -0.5
        col = lax.axis_index("col")
        z, quad = col // 4, col % 4
        norm = jnp.transpose(log_norm, (2, 1, 0)).reshape(48, 64)
        mask = lax.dynamic_slice(pair_mask, (4 * quad, z * 192), (4, 192))
        added = jnp.where(mask == 1, 0.0, -BIG).astype(BF16)
        added = jnp.broadcast_to(added[:, :, None], (4, 192, 128))
        bias = jnp.transpose(pair_bias, (1, 0, 2)).reshape(48, 768)
        vmem = pl.BlockSpec(memory_space=pltpu.VMEM)
        dma = pltpu.SemaphoreType.DMA
        grad_query, grad_key, grad_value, grad_bias = pl.pallas_call(
            functools.partial(kernel, (ny, nxh, nz), scaling),
            out_shape=(
                jax.ShapeDtypeStruct((16, 48, 128), BF16),
                jax.ShapeDtypeStruct((16, 48, 128), BF16),
                jax.ShapeDtypeStruct((16, 48, 128), BF16),
                jax.ShapeDtypeStruct((48, 768), BF16),
            ),
            in_specs=[vmem] * 8,
            out_specs=(vmem,) * 4,
            scratch_shapes=[
                pltpu.VMEM((nz, 4, 2, 2, 96, 128), BF16),
                pltpu.VMEM((nz, 2, 96, 128), BF16),
                pltpu.VMEM((4, 48, 128), BF16),
                pltpu.VMEM((4, 192, 128), BF16),
                pltpu.VMEM((4, 192, 128), BF16),
                pltpu.VMEM((4, 768, 256), BF16),
                pltpu.VMEM((4, 768, 256), BF16),
                pltpu.VMEM((nz, 2, 2, 48, 768), BF16),
                pltpu.VMEM((nz + 1, 4, 2, 96, 128), BF16),
                pltpu.VMEM((nz, 4, 2, 96, 128), BF16),
                pltpu.VMEM((4, 192, 128), F32),
                pltpu.VMEM((4, 3, 64, 256), F32),
                pltpu.VMEM((4, 3, 64, 256), F32),
                pltpu.VMEM((nz, 192, 768), F32),
                pltpu.VMEM((3, 4, 192, 128), BF16),
                pltpu.VMEM((nz, 2, 2, 48, 768), BF16),
                pltpu.VMEM((nz, 2, 48, 768), BF16),
                pltpu.VMEM((nz, 2, 48, 768), BF16),
                pltpu.VMEM((ny - 1, nxh, 2, 48, 768), BF16),
                pltpu.VMEM((nxh, 2, 48, 768), BF16),
                pltpu.VMEM((nx - 1, 48, 768), BF16),
                pltpu.VMEM((48, 768), BF16),
                dma((5, 3)), dma((5, 3)), dma((5,)),
                dma((nz, 4, 2)), dma((nz, 4, 2)),
                dma((nz, 2)), dma((nz, 2)),
                dma((nz, 4, 2)), dma((nz + 1, 4, 2)),
                dma((17,)), dma((17,)),
                dma((17,)), dma((17,)),
                dma((3, 3)), dma((3, 3)), dma((3,)),
                dma((2,)),
            ],
            compiler_params=pltpu.CompilerParams(
                collective_id=0, has_side_effects=True, vmem_limit_bytes=56 * 1024 * 1024
            ),
        )(query_proj, key_proj, value_proj, attn_out, out_grad, norm, added, bias)
        grad_bias = jnp.transpose(grad_bias.reshape(48, HEADS, 192), (1, 0, 2))
        return grad_query, grad_key, grad_value, grad_bias

    placed = (
        P("row", "col", None), P("row", "col", None), P("row", "col", None), P("row", "col", None),
        P("row", "col", None), P(None, "row", "col"), P("row", None), P(None, "col", "row"),
    )
    return jax.shard_map(
        shards,
        mesh=mesh,
        in_specs=placed,
        out_specs=(P("row", "col", None), P("row", "col", None), P("row", "col", None), P(None, "col", "row")),
        check_vma=False,
    )
```

```python
import functools

import jax
import jax.numpy as jnp
from jax import lax
from jax.experimental import pallas as pl
from jax.experimental.pallas import tpu as pltpu
from jax.sharding import PartitionSpec as P

MESH = pl.DeviceIdType.MESH
HEADS = 4
BIG = 1.0e30
F32 = jnp.float32
BF16 = jnp.bfloat16
NT = (((1,), (1,)), ((), ()))
TN = (((0,), (0,)), ((), ()))


def iota(shape, axis):
    return lax.broadcasted_iota(jnp.int32, shape, axis)


def split3(value):
    high = value.astype(BF16).astype(F32)
    rest = value - high
    middle = rest.astype(BF16).astype(F32)
    low = (rest - middle).astype(BF16).astype(F32)
    return high, middle, low


def kernel(
    geometry, scaling,
    q_ref, k_ref, v_ref, o_ref, g_ref, ln_ref, mask_ref, bias_ref,
    dq_out, dk_out, dv_out, db_out,
    o_own, g_own, ln_own, mask_own, bias_own, bias_wide,
    qg, st, st_out, kx, vx, ws, wp, bias_all,
    acc_in, acc_out, dq_own, dk_acc, dv_acc, db_acc,
    back, db_send, db_core, db_keep, db_y, db_ysum, db_x, db_home,
    load, qg_send, qg_recv, qg_local, kv_send, kv_recv, kv_local, t_send, t_recv, t_local,
    r_send, r_recv, s_send, s_recv, a_send, a_recv,
    bx_send, bx_recv, by_send, by_recv, bc_send, bc_recv,
    dc_send, dc_recv, dy_send, dy_recv, dx_send, dx_recv,
    e_send, e_recv, e_local, h_local,
):
    ny, nxh, nz = geometry
    nx = 2 * nxh
    row = lax.axis_index("row")
    col = lax.axis_index("col")
    y, xh = lax.div(row, nxh), lax.rem(row, nxh)
    z, quad = lax.div(col, 4), lax.rem(col, 4)
    xl, core = lax.div(quad, 2), lax.rem(quad, 2)
    x = xh * 2 + xl
    right, left = lax.rem(z + 1, nz), lax.rem(z + nz - 1, nz)
    right_id = {"col": right * 4 + quad}
    left_id = {"col": left * 4 + quad}
    quad_of = [lax.rem(quad + o, 4) for o in range(1, 4)]
    quad_ids = [{"col": z * 4 + p} for p in quad_of]
    xs = [lax.rem(x + o, nx) for o in range(1, nx)]
    x_ids = [
        {"row": y * nxh + lax.div(p, 2), "col": z * 4 + lax.rem(p, 2) * 2 + core} for p in xs
    ]
    ys = [lax.rem(y + o, ny) for o in range(1, ny)]
    y_ids = [{"row": p * nxh + xh} for p in ys]
    core_id = {"col": z * 4 + xl * 2 + 1 - core}
    first = xl == 0
    source_step = jnp.where(first, lax.rem(row - z + nz, nz), lax.rem(z - row + nz, nz))
    to_plane = {"row": source_step, "col": row * 4 + quad}
    home_z = jnp.where(first, lax.rem(z - row + nz, nz), lax.rem(z + row, nz))
    to_home = {"row": z, "col": home_z * 4 + quad}
    alone = jnp.logical_and(row == 0, z == 0)

    loads = [
        pltpu.make_async_copy(source, target, load.at[at])
        for at, (source, target) in enumerate(
            [(bias_ref, bias_own), (g_ref, g_own), (o_ref, o_own), (ln_ref, ln_own), (mask_ref, mask_own)]
        )
    ]
    for copy in loads:
        copy.start()

    barrier = pltpu.get_barrier_semaphore()
    greeted = quad_ids + [right_id, left_id] + x_ids + y_ids
    for peer in greeted:
        pl.semaphore_signal(barrier, inc=1, device_id=peer, device_id_type=MESH)

    @pl.when(jnp.logical_not(alone))
    def _():
        pl.semaphore_signal(barrier, inc=1, device_id=to_plane, device_id_type=MESH)
        pl.semaphore_signal(barrier, inc=1, device_id=to_home, device_id_type=MESH)

    loads[0].wait()
    bias_wide[...] = jnp.concatenate([bias_own[h] for h in range(HEADS)], axis=1)

    pl.semaphore_wait(barrier, len(greeted) + jnp.where(alone, 0, 2))

    def remote(source, target, send, recv, device):
        return pltpu.make_async_remote_copy(
            src_ref=source, dst_ref=target, send_sem=send, recv_sem=recv,
            device_id=device, device_id_type=MESH,
        )

    bias_mine = bias_all.at[row, core, xl]
    bias_push = remote(
        bias_wide, bias_all.at[source_step, core, xl], bx_send.at[0], bx_recv.at[0], to_plane
    )
    bias_self = pltpu.make_async_copy(bias_wide, bias_mine, h_local.at[0])

    @pl.when(jnp.logical_not(alone))
    def _():
        bias_push.start()

    @pl.when(alone)
    def _():
        bias_self.start()

    place = pl.ds(pl.multiple_of(core * 48, 48), 48)
    mine = pl.ds(pl.multiple_of(quad * 48, 48), 48)

    def swap_row(i):
        copies = []
        for at, source in enumerate((q_ref, g_ref)):
            target = qg.at[0, i, xl, at, place, :]
            for o in range(3):
                copies.append(remote(
                    source.at[4 * quad_of[o] + i], target,
                    qg_send.at[at, i, o], qg_recv.at[at, i, o], quad_ids[o],
                ))
            copies.append(pltpu.make_async_copy(source.at[4 * quad + i], target, qg_local.at[at, i]))
        return copies

    for i in range(4):
        for copy in swap_row(i):
            copy.start()
    swaps = []
    for at, (source, target) in enumerate(((k_ref, kx.at[:, mine, :]), (v_ref, vx.at[:, mine, :]))):
        for o in range(3):
            swaps.append(remote(
                source.at[pl.ds(4 * quad_of[o], 4)], target, kv_send.at[at, o], kv_recv.at[at, o], quad_ids[o],
            ))
        swaps.append(pltpu.make_async_copy(source.at[pl.ds(4 * quad, 4)], target, kv_local.at[at]))
    for copy in swaps:
        copy.start()

    def pass_on(s, i):
        return [
            remote(qg.at[s, i, 0], qg.at[s + 1, i, 0], r_send.at[s, i, 0], r_recv.at[s + 1, i, 0], right_id),
            remote(qg.at[s, i, 1], qg.at[s + 1, i, 1], r_send.at[s, i, 1], r_recv.at[s + 1, i, 1], left_id),
        ]

    def pass_stats(s):
        return [
            remote(st.at[s, 0], st.at[s + 1, 0], s_send.at[s, 0], s_recv.at[s + 1, 0], right_id),
            remote(st.at[s, 1], st.at[s + 1, 1], s_send.at[s, 1], s_recv.at[s + 1, 1], left_id),
        ]

    def pass_sum(s, i):
        return [
            remote(acc_out.at[s, i, 0], acc_in.at[s + 1, i, 0], a_send.at[s, i, 0], a_recv.at[s + 1, i, 0], right_id),
            remote(acc_out.at[s, i, 1], acc_in.at[s + 1, i, 1], a_send.at[s, i, 1], a_recv.at[s + 1, i, 1], left_id),
        ]

    for copy in loads[1:]:
        copy.wait()
    lane = iota((48, 128), 1)
    term = lax.rem(lane, 8)
    norm = jnp.concatenate([ln_own[h] for h in range(HEADS)], axis=0) * F32(scaling ** -1)
    norm_terms = [part.astype(BF16) for part in split3(norm)]
    source_lane, target_lane = iota((128, 128), 0), iota((128, 128), 1)
    target_term = lax.rem(target_lane, 8)
    same_head = lax.div(source_lane, 32) == lax.rem(lax.div(target_lane, 8), 4)
    delta_term = jnp.logical_and(target_term >= 3, target_term < 6)
    norm_source, norm_target = iota((64, 128), 0), iota((64, 128), 1)
    norm_row = lax.rem(norm_source, 16)
    norm_fits = jnp.logical_and(
        lax.rem(norm_target, 8) < 3, lax.div(norm_source, 16) == lax.rem(lax.div(norm_target, 8), 4)
    )

    def stats(target, carry):
        total = jnp.zeros((48, 128), F32)
        pick = jnp.where(
            jnp.logical_and(norm_row - target * 4 == lax.div(norm_target, 32), norm_fits), 1.0, 0.0
        ).astype(BF16)
        for part in norm_terms:
            total += lax.dot_general(part, pick, TN, preferred_element_type=F32)
        for i in range(4):
            gather = jnp.where(
                jnp.logical_and(
                    jnp.logical_and(same_head, delta_term), lax.div(target_lane, 32) == i
                ), 1.0, 0.0,
            ).astype(BF16)
            product = g_own[target * 4 + i].astype(F32) * o_own[target * 4 + i].astype(F32)
            high = product.astype(BF16)
            low = (product - high.astype(F32)).astype(BF16)
            total += jnp.dot(high, gather, preferred_element_type=F32)
            total += jnp.dot(low, gather, preferred_element_type=F32)
        high, middle, low = split3(-total)
        value = jnp.where(
            jnp.logical_or(term == 0, term == 3), high,
            jnp.where(jnp.logical_or(term == 1, term == 4), middle,
                      jnp.where(jnp.logical_or(term == 2, term == 5), low,
                                jnp.where(term == 6, 1.0, 0.0))),
        )
        st_out[target] = value.astype(BF16)
        return carry

    lax.fori_loop(0, 4, stats, 0)
    target = st.at[0, xl, place, :]
    stat_swaps = [
        remote(st_out.at[quad_of[o]], target, t_send.at[o], t_recv.at[o], quad_ids[o]) for o in range(3)
    ]
    stat_swaps.append(pltpu.make_async_copy(st_out.at[quad], target, t_local.at[0]))
    for copy in stat_swaps:
        copy.start()

    def start_row(i):
        for copy in swap_row(i):
            copy.wait()
        for copy in pass_on(0, i):
            copy.start()

    start_row(0)

    @pl.when(jnp.logical_not(alone))
    def _():
        bias_push.wait()

    @pl.when(alone)
    def _():
        bias_self.wait()

    bias_copies = []
    for o in range(nx - 1):
        copy = remote(bias_mine, bias_mine, bx_send.at[1 + o], bx_recv.at[1 + o], x_ids[o])
        copy.start()
        bias_copies.append(copy)

    start_row(1)
    start_row(2)
    start_row(3)
    for copy in stat_swaps:
        copy.wait()
    for copy in pass_stats(0):
        copy.start()

    for copy in bias_copies:
        copy.wait()

    def bias_y(o, a):
        part = bias_all.at[y * nxh + a, core]
        return remote(part, part, by_send.at[o, a], by_recv.at[o, a], y_ids[o])

    for a in range(nxh):
        for o in range(ny - 1):
            bias_y(o, a).start()
    for copy in swaps:
        copy.wait()

    wide_lane = iota((192, 128), 1)
    masked = mask_own[:, 0:192]
    for other in range(1, nz):
        masked = jnp.where(z == other, mask_own[:, 192 * other:192 * other + 192], masked)
    masked = jnp.where(masked == 1, 0.0, -BIG).astype(BF16)
    mask_row, mask_lane = iota((16, 128), 0), iota((16, 128), 1)

    def weights(i, carry):
        keys, values = kx[i].astype(F32), vx[i].astype(F32)
        pick = jnp.where(
            jnp.logical_and(mask_row == 4 * quad + i, lax.rem(mask_lane, 8) == 6), 1.0, 0.0
        ).astype(BF16)
        mask_lanes = lax.dot_general(masked, pick, TN, preferred_element_type=F32)
        zero = jnp.zeros((192, 128), F32)
        for h in range(HEADS):
            head = lax.div(wide_lane, 32) == h
            block = pl.ds(h * 192, 192)
            offset = wide_lane - (i * 32 + h * 8)
            ws[i, block, 0:128] = jnp.where(head, keys, zero).astype(BF16)
            wp[i, block, 0:128] = jnp.where(head, values, zero).astype(BF16)
            ws[i, block, 128:256] = jnp.where(
                jnp.logical_and(offset >= 0, offset < 3), 1.0, jnp.where(offset == 6, mask_lanes, zero)
            ).astype(BF16)
            wp[i, block, 128:256] = jnp.where(
                jnp.logical_and(offset >= 3, offset < 6), 1.0, zero
            ).astype(BF16)
        dk_acc[i] = jnp.zeros(dk_acc.shape[1:], F32)
        dv_acc[i] = jnp.zeros(dv_acc.shape[1:], F32)
        return carry

    lax.fori_loop(0, 4, weights, 0)

    def bias_core(s):
        part = bias_all.at[s, core]
        return remote(part, part, bc_send.at[s], bc_recv.at[s], core_id)

    def share_bias(s):
        o = lax.rem(y - lax.div(s, nxh) + ny, ny)

        @pl.when(o > 0)
        def _():
            part = bias_all.at[s, core]
            a = lax.rem(s, nxh)
            remote(part, part, by_send.at[o - 1, a], by_recv.at[o - 1, a], core_id).wait_recv()

        bias_core(s).start()

    share_bias(0)

    def sum_core(s):
        return remote(db_send.at[s], db_core.at[s], dc_send.at[s], dc_recv.at[s], core_id)

    def sum_y(s):
        o = lax.rem(lax.div(s, nxh) - y + ny, ny)
        a = lax.rem(s, nxh)
        at = jnp.where(o > 0, o - 1, 0)
        return o, remote(
            db_keep.at[s], db_y.at[at, a], dy_send.at[s], dy_recv.at[at, a],
            {"row": lax.div(s, nxh) * nxh + xh},
        )

    def share_sum(s):
        for w in range(2):
            rows = pl.ds(pl.multiple_of(w * 96 + (1 - core) * 48, 48), 48)
            db_send[s, w] = db_acc[s, rows, :].astype(BF16)
        sum_core(s).start()

    def add_cores(s):
        sum_core(s).wait_recv()
        for w in range(2):
            rows = pl.ds(pl.multiple_of(w * 96 + core * 48, 48), 48)
            whole = db_acc[s, rows, :] + db_core[s, w].astype(F32)
            db_acc[s, rows, :] = whole
            db_keep[s, w] = whole.astype(BF16)
        o, copy = sum_y(s)

        @pl.when(o > 0)
        def _():
            copy.start()

    def turned(acc, i, factor):
        blocks = []
        for t in range(3):
            unit = jnp.where(iota((64, 128), 0) + 32 * t == iota((64, 128), 1), 1.0, 0.0).astype(BF16)
            part = (acc[i, t] * F32(factor)).astype(BF16)
            blocks.append(lax.dot_general(part, unit, TN, preferred_element_type=F32))
        stacked = jnp.concatenate(blocks, axis=0)
        total = jnp.zeros((192, 128), F32)
        for h in range(HEADS):
            total = jnp.where(lax.div(wide_lane, 32) == h, stacked[192 * h:192 * h + 192], total)
        return total.astype(BF16)

    outs = (dq_out, dk_out, dv_out)

    def give_back(at, i):
        copies = []
        for o in range(3):
            columns = pl.ds(pl.multiple_of(quad_of[o] * 48, 48), 48)
            copies.append(remote(
                back.at[at, i, columns, :], outs[at].at[4 * quad + i],
                e_send.at[at, i, o], e_recv.at[at, i, o], quad_ids[o],
            ))
        copies.append(pltpu.make_async_copy(back.at[at, i, mine, :], outs[at].at[4 * quad + i], e_local.at[at, i]))
        return copies

    def one_row(s, i):
        queries = jnp.concatenate([qg[s, i, 0, 0], qg[s, i, 1, 0]], axis=0)
        grads = jnp.concatenate([qg[s, i, 0, 1], qg[s, i, 1, 1]], axis=0)
        terms = jnp.concatenate([st[s, 0], st[s, 1]], axis=0)
        left_s = jnp.concatenate([queries, terms], axis=1)
        left_p = jnp.concatenate([grads, terms], axis=1)
        queries_t, grads_t = queries.T, grads.T
        grad_query = jnp.zeros((192, 128), F32)
        for t in range(3):
            span = pl.ds(256 * t, 256)
            logits = lax.dot_general(left_s, ws[i, span, :], NT, preferred_element_type=F32)
            prob_grad = lax.dot_general(left_p, wp[i, span, :], NT, preferred_element_type=F32)
            bias = jnp.concatenate(
                [bias_all[s, c, w, :, span] for w in range(2) for c in range(2)], axis=0
            ).astype(F32)
            probs = jnp.exp(logits * F32(scaling) + bias)
            score_grad = probs * prob_grad
            probs_low = probs.astype(BF16)
            score_low = score_grad.astype(BF16)

            @pl.when(i == 0)
            def _():
                db_acc[s, :, span] = score_grad

            @pl.when(i > 0)
            def _():
                db_acc[s, :, span] += score_grad

            grad_query += jnp.dot(score_low, ws[i, span, 0:128], preferred_element_type=F32)
            part = slice(32 * t, 32 * t + 64)
            dk_acc[i, t] += jnp.dot(queries_t[part], score_low, preferred_element_type=F32)
            dv_acc[i, t] += jnp.dot(grads_t[part], probs_low, preferred_element_type=F32)

        @pl.when(s < nz - 1)
        def _():
            for copy in pass_on(s, i):
                copy.wait_recv()

            @pl.when(s < nz - 2)
            def _():
                for copy in pass_on(s + 1, i):
                    copy.start()

        @pl.when(s == 0)
        def _():
            dq_own[i] = grad_query

        @pl.when(s == 1)
        def _():
            acc_out[1, i, 0] = grad_query[:96].astype(BF16)
            acc_out[1, i, 1] = grad_query[96:].astype(BF16)

        @pl.when(s > 1)
        def _():
            for copy in pass_sum(s - 1, i):
                copy.wait_recv()
            acc_out[s, i, 0] = (grad_query[:96] + acc_in[s, i, 0].astype(F32)).astype(BF16)
            acc_out[s, i, 1] = (grad_query[96:] + acc_in[s, i, 1].astype(F32)).astype(BF16)

        @pl.when(s > 0)
        def _():
            for copy in pass_sum(s, i):
                copy.start()

        @pl.when(s == nz - 1)
        def _():
            back[1, i] = turned(dk_acc, i, scaling)
            back[2, i] = turned(dv_acc, i, 1.0)
            for at in (1, 2):
                for copy in give_back(at, i):
                    copy.start()

    def one_step(s, carry):
        bias_core(s).wait_recv()

        def rows(i, inner):
            one_row(s, i)

            @pl.when(jnp.logical_and(i == 1, s > 0))
            def _():
                add_cores(s - 1)

            @pl.when(jnp.logical_and(i == 2, s < nz - 1))
            def _():
                share_bias(s + 1)

            return inner

        lax.fori_loop(0, 4, rows, 0)
        share_sum(s)

        @pl.when(s < nz - 1)
        def _():
            for copy in pass_stats(s):
                copy.wait_recv()

            @pl.when(s < nz - 2)
            def _():
                for copy in pass_stats(s + 1):
                    copy.start()

        return carry

    lax.fori_loop(0, nz, one_step, 0)

    def finish_query(i, carry):
        for copy in pass_sum(nz - 1, i):
            copy.wait_recv()
        for w in range(2):
            part = pl.ds(96 * w, 96)
            whole = dq_own[i, part, :] + acc_in[nz, i, w].astype(F32)
            back[0, i, part, :] = (whole * F32(scaling)).astype(BF16)
        for copy in give_back(0, i):
            copy.start()
        return carry

    add_cores(nz - 1)
    lax.fori_loop(0, 4, finish_query, 0)

    for a in range(nxh):
        for o in range(ny - 1):
            remote(db_keep.at[0], db_y.at[o, a], dy_send.at[0], dy_recv.at[o, a], y_ids[o]).wait_recv()
    for a in range(nxh):
        for w in range(2):
            rows = pl.ds(pl.multiple_of(w * 96 + core * 48, 48), 48)
            whole = db_acc[y * nxh + a, rows, :]
            for o in range(ny - 1):
                whole = whole + db_y[o, a, w].astype(F32)
            db_acc[y * nxh + a, rows, :] = whole
            db_ysum[a, w] = whole.astype(BF16)
    copies = []
    for o in range(nx - 1):
        copy = remote(
            db_ysum.at[lax.div(xs[o], 2), lax.rem(xs[o], 2)], db_x.at[o],
            dx_send.at[1 + o], dx_recv.at[1 + o], x_ids[o],
        )
        copy.start()
        copies.append(copy)
    for copy in copies:
        copy.wait()
    whole = db_acc[row, pl.ds(pl.multiple_of(xl * 96 + core * 48, 48), 48), :]
    for o in range(nx - 1):
        whole = whole + db_x[o].astype(F32)
    for h in range(HEADS):
        db_home[h] = whole[:, 192 * h:192 * h + 192].astype(BF16)
    home_push = remote(db_home, db_out, dx_send.at[0], dx_recv.at[0], to_home)
    home_self = pltpu.make_async_copy(db_home, db_out, h_local.at[1])

    @pl.when(jnp.logical_not(alone))
    def _():
        home_push.start()

    @pl.when(alone)
    def _():
        home_self.start()

    def sent(s, carry):
        def rows(i, inner):
            @pl.when(s < nz - 1)
            def _():
                for copy in pass_on(s, i):
                    copy.wait_send()

            @pl.when(s > 0)
            def _():
                for copy in pass_sum(s, i):
                    copy.wait_send()

            return inner

        lax.fori_loop(0, 4, rows, 0)

        @pl.when(s < nz - 1)
        def _():
            for copy in pass_stats(s):
                copy.wait_send()

        bias_core(s).wait_send()
        sum_core(s).wait_send()
        o, copy = sum_y(s)

        @pl.when(o > 0)
        def _():
            copy.wait_send()

        return carry

    lax.fori_loop(0, nz, sent, 0)
    for a in range(nxh):
        for o in range(ny - 1):
            bias_y(o, a).wait_send()

    def returned(i, carry):
        for at in range(3):
            for copy in give_back(at, i):
                copy.wait()
        return carry

    lax.fori_loop(0, 4, returned, 0)

    @pl.when(jnp.logical_not(alone))
    def _():
        home_push.wait()

    @pl.when(alone)
    def _():
        home_self.wait()


def hand_on(*refs):
    copies = [pltpu.make_async_copy(refs[at], refs[4 + at], refs[8].at[at]) for at in range(4)]
    for copy in copies:
        copy.start()
    for copy in copies:
        copy.wait()


def solution(mesh):
    rows_n, cols_n = mesh.shape["row"], mesh.shape["col"]
    nz = cols_n // 4
    nxh = 2 if rows_n >= 4 else 1
    ny = rows_n // nxh
    nx = 2 * nxh

    def shards(query_proj, key_proj, value_proj, attn_out, out_grad, log_norm, pair_mask, pair_bias):
        width = query_proj.shape[2]
        scaling = (width // HEADS) ** -0.5
        anywhere = pl.BlockSpec(memory_space=pl.ANY)
        dma = pltpu.SemaphoreType.DMA
        shapes = (
            jax.ShapeDtypeStruct((16, 48, 128), BF16),
            jax.ShapeDtypeStruct((16, 48, 128), BF16),
            jax.ShapeDtypeStruct((16, 48, 128), BF16),
            jax.ShapeDtypeStruct((HEADS, 48, 192), BF16),
        )
        results = pl.pallas_call(
            functools.partial(kernel, (ny, nxh, nz), scaling),
            out_shape=shapes,
            in_specs=[anywhere] * 8,
            out_specs=(anywhere,) * 4,
            scratch_shapes=[
                pltpu.VMEM((16, 48, 128), BF16),
                pltpu.VMEM((16, 48, 128), BF16),
                pltpu.VMEM((HEADS, 16, 48), F32),
                pltpu.VMEM((16, nz * 192), jnp.int32),
                pltpu.VMEM((HEADS, 48, 192), BF16),
                pltpu.VMEM((48, 768), BF16),
                pltpu.VMEM((nz, 4, 2, 2, 96, 128), BF16),
                pltpu.VMEM((nz, 2, 96, 128), BF16),
                pltpu.VMEM((4, 48, 128), BF16),
                pltpu.VMEM((4, 192, 128), BF16),
                pltpu.VMEM((4, 192, 128), BF16),
                pltpu.VMEM((4, 768, 256), BF16),
                pltpu.VMEM((4, 768, 256), BF16),
                pltpu.VMEM((nz, 2, 2, 48, 768), BF16),
                pltpu.VMEM((nz + 1, 4, 2, 96, 128), BF16),
                pltpu.VMEM((nz, 4, 2, 96, 128), BF16),
                pltpu.VMEM((4, 192, 128), F32),
                pltpu.VMEM((4, 3, 64, 256), F32),
                pltpu.VMEM((4, 3, 64, 256), F32),
                pltpu.VMEM((nz, 192, 768), F32),
                pltpu.VMEM((3, 4, 192, 128), BF16),
                pltpu.VMEM((nz, 2, 48, 768), BF16),
                pltpu.VMEM((nz, 2, 48, 768), BF16),
                pltpu.VMEM((nz, 2, 48, 768), BF16),
                pltpu.VMEM((ny - 1, nxh, 2, 48, 768), BF16),
                pltpu.VMEM((nxh, 2, 48, 768), BF16),
                pltpu.VMEM((nx - 1, 48, 768), BF16),
                pltpu.VMEM((HEADS, 48, 192), BF16),
                dma((5,)),
                dma((2, 4, 3)), dma((2, 4, 3)), dma((2, 4)),
                dma((2, 3)), dma((2, 3)), dma((2,)),
                dma((3,)), dma((3,)), dma((1,)),
                dma((nz, 4, 2)), dma((nz, 4, 2)),
                dma((nz, 2)), dma((nz, 2)),
                dma((nz, 4, 2)), dma((nz + 1, 4, 2)),
                dma((nx,)), dma((nx,)),
                dma((ny - 1, nxh)), dma((ny - 1, nxh)),
                dma((nz,)), dma((nz,)),
                dma((nz,)), dma((nz,)),
                dma((nz,)), dma((ny - 1, nxh)),
                dma((nx,)), dma((nx,)),
                dma((3, 4, 3)), dma((3, 4, 3)), dma((3, 4)),
                dma((2,)),
            ],
            compiler_params=pltpu.CompilerParams(
                collective_id=0, has_side_effects=True, vmem_limit_bytes=56 * 1024 * 1024
            ),
        )(query_proj, key_proj, value_proj, attn_out, out_grad, log_norm, pair_mask, pair_bias)
        return pl.pallas_call(
            hand_on,
            out_shape=shapes,
            in_specs=[anywhere] * 4,
            out_specs=(anywhere,) * 4,
            scratch_shapes=[dma((4,))],
        )(*results)

    placed = (
        P("row", "col", None), P("row", "col", None), P("row", "col", None), P("row", "col", None),
        P("row", "col", None), P(None, "row", "col"), P("row", None), P(None, "col", "row"),
    )
    return jax.shard_map(
        shards,
        mesh=mesh,
        in_specs=placed,
        out_specs=(P("row", "col", None), P("row", "col", None), P("row", "col", None), P(None, "col", "row")),
        check_vma=False,
    )
```

```python
import functools

import jax
import jax.numpy as jnp
from jax import lax
from jax.experimental import pallas as pl
from jax.experimental.pallas import tpu as pltpu
from jax.sharding import PartitionSpec as P

MESH = pl.DeviceIdType.MESH
HEADS = 4
BIG = 1.0e30
F32 = jnp.float32
BF16 = jnp.bfloat16
NT = (((1,), (1,)), ((), ()))
TN = (((0,), (0,)), ((), ()))


def iota(shape, axis):
    return lax.broadcasted_iota(jnp.int32, shape, axis)


def split3(value):
    high = value.astype(BF16).astype(F32)
    rest = value - high
    middle = rest.astype(BF16).astype(F32)
    low = (rest - middle).astype(BF16).astype(F32)
    return high, middle, low


def kernel(
    geometry, scaling,
    q_ref, k_ref, v_ref, o_ref, g_ref, ln_ref, mask_ref, bias_ref,
    dq_out, dk_out, dv_out, db_out,
    o_own, g_own, ln_own, mask_own, bias_own, bias_wide,
    qg, st, st_out, kx, vx, ws, wp, bias_all,
    acc_in, acc_out, dq_own, dk_acc, dv_acc, db_acc,
    back, db_send, db_core, db_keep, db_owned, db_parts, db_whole, db_home, db_final,
    load, qg_send, qg_recv, qg_local, t_send, t_recv, t_local,
    r_send, r_recv, s_send, s_recv, a_send, a_recv,
    bp_send, bp_recv, by_send, by_recv, bc_send, bc_recv,
    dc_send, dc_recv, do_send, do_recv, dp_recv, dh_send, dh_recv,
    e_send, e_recv, e_local, h_local,
):
    ny, nxh, nz = geometry
    nx = 2 * nxh
    row = lax.axis_index("row")
    col = lax.axis_index("col")
    y, xh = lax.div(row, nxh), lax.rem(row, nxh)
    z, quad = lax.div(col, 4), lax.rem(col, 4)
    xl, core = lax.div(quad, 2), lax.rem(quad, 2)
    x = xh * 2 + xl
    right, left = lax.rem(z + 1, nz), lax.rem(z + nz - 1, nz)
    right_id = {"col": right * 4 + quad}
    left_id = {"col": left * 4 + quad}
    quad_of = [lax.rem(quad + o, 4) for o in range(1, 4)]
    quad_ids = [{"col": z * 4 + p} for p in quad_of]
    plane_ids = []
    for o in range(1, nx * ny):
        px, py = lax.rem(x + o % nx, nx), lax.rem(y + o // nx, ny)
        plane_ids.append({"row": py * nxh + lax.div(px, 2), "col": z * 4 + lax.rem(px, 2) * 2 + core})
    core_id = {"col": z * 4 + xl * 2 + 1 - core}
    own_step = lax.rem(row - z + nz, nz)
    home_step = jnp.where(xl == 0, own_step, lax.rem(z - row + nz, nz))
    to_owner = {"row": lax.rem(row + home_step, nz), "col": row * 4 + quad}

    def home_of(s, w):
        return {"row": z, "col": lax.rem(z + (s if w else nz - s), nz) * 4 + w * 2 + core}

    home_z = lax.rem(jnp.where(xl == 0, z + nz - own_step, z + own_step), nz)
    to_home = {"row": z, "col": home_z * 4 + quad}
    alone = row == z
    last = nz - (2 if nz > 2 else 1)

    loads = [
        pltpu.make_async_copy(source, target, load.at[at])
        for at, (source, target) in enumerate(
            [(bias_ref, bias_own), (g_ref, g_own), (o_ref, o_own), (ln_ref, ln_own), (mask_ref, mask_own)]
        )
    ]
    for copy in loads:
        copy.start()

    barrier = pltpu.get_barrier_semaphore()
    greeted = quad_ids + [right_id, left_id] + plane_ids
    for peer in greeted:
        pl.semaphore_signal(barrier, inc=1, device_id=peer, device_id_type=MESH)

    @pl.when(jnp.logical_not(alone))
    def _():
        pl.semaphore_signal(barrier, inc=1, device_id=to_owner, device_id_type=MESH)
        pl.semaphore_signal(barrier, inc=1, device_id=to_home, device_id_type=MESH)

    @pl.when(home_step >= last)
    def _():
        for other in range(ny * nxh):
            for w in range(2):
                pl.semaphore_signal(
                    barrier, inc=1, device_id={"row": other, "col": row * 4 + w * 2 + core},
                    device_id_type=MESH,
                )

    loads[0].wait()
    bias_wide[...] = jnp.concatenate([bias_own[h] for h in range(HEADS)], axis=1)

    pl.semaphore_wait(barrier, len(greeted) + 2 * (nz - last) + jnp.where(alone, 0, 2))

    def remote(source, target, send, recv, device):
        return pltpu.make_async_remote_copy(
            src_ref=source, dst_ref=target, send_sem=send, recv_sem=recv,
            device_id=device, device_id_type=MESH,
        )

    place = pl.ds(pl.multiple_of(core * 48, 48), 48)
    mine = pl.ds(pl.multiple_of(quad * 48, 48), 48)

    def swap_row(i, sources):
        copies = []
        for at, source in sources:
            target = (qg.at[0, i, xl, at, place, :] if at < 2 else (kx, vx)[at - 2].at[i, mine, :])
            for o in range(3):
                copies.append(remote(
                    source.at[4 * quad_of[o] + i], target,
                    qg_send.at[at, i, o], qg_recv.at[at, i, o], quad_ids[o],
                ))
            copies.append(pltpu.make_async_copy(source.at[4 * quad + i], target, qg_local.at[at, i]))
        return copies

    queries_grads = ((0, q_ref), (1, g_ref))
    keys_values = ((2, k_ref), (3, v_ref))
    for copy in swap_row(0, queries_grads + keys_values):
        copy.start()

    bias_mine = bias_all.at[own_step, core, xl]
    bias_push = remote(
        bias_wide, bias_all.at[home_step, core, xl], bp_send.at[0], bp_recv.at[0], to_owner
    )

    def spread():
        return [
            remote(bias_mine, bias_mine, by_send.at[o], by_recv.at[own_step, xl], peer)
            for o, peer in enumerate(plane_ids)
        ]

    @pl.when(alone)
    def _():
        bias_all[0, core, xl] = bias_wide[...]
        for copy in spread():
            copy.start()

    @pl.when(jnp.logical_not(alone))
    def _():
        bias_push.start()

    for i in range(1, 4):
        for copy in swap_row(i, queries_grads + keys_values):
            copy.start()

    def pass_on(s, i):
        return [
            remote(qg.at[s, i, 0], qg.at[s + 1, i, 0], r_send.at[s, i, 0], r_recv.at[s + 1, i, 0], right_id),
            remote(qg.at[s, i, 1], qg.at[s + 1, i, 1], r_send.at[s, i, 1], r_recv.at[s + 1, i, 1], left_id),
        ]

    def pass_stats(s):
        return [
            remote(st.at[s, 0], st.at[s + 1, 0], s_send.at[s, 0], s_recv.at[s + 1, 0], right_id),
            remote(st.at[s, 1], st.at[s + 1, 1], s_send.at[s, 1], s_recv.at[s + 1, 1], left_id),
        ]

    def pass_sum(s, i):
        return [
            remote(acc_out.at[s, i, 0], acc_in.at[s + 1, i, 0], a_send.at[s, i, 0], a_recv.at[s + 1, i, 0], right_id),
            remote(acc_out.at[s, i, 1], acc_in.at[s + 1, i, 1], a_send.at[s, i, 1], a_recv.at[s + 1, i, 1], left_id),
        ]

    for copy in loads[1:]:
        copy.wait()
    lane = iota((48, 128), 1)
    term = lax.rem(lane, 8)
    norm = jnp.concatenate([ln_own[h] for h in range(HEADS)], axis=0) * F32(scaling ** -1)
    norm_terms = [part.astype(BF16) for part in split3(norm)]
    source_lane, target_lane = iota((128, 128), 0), iota((128, 128), 1)
    target_term = lax.rem(target_lane, 8)
    same_head = lax.div(source_lane, 32) == lax.rem(lax.div(target_lane, 8), 4)
    delta_term = jnp.logical_and(target_term >= 3, target_term < 6)
    norm_source, norm_target = iota((64, 128), 0), iota((64, 128), 1)
    norm_row = lax.rem(norm_source, 16)
    norm_fits = jnp.logical_and(
        lax.rem(norm_target, 8) < 3, lax.div(norm_source, 16) == lax.rem(lax.div(norm_target, 8), 4)
    )

    def stats(target, carry):
        total = jnp.zeros((48, 128), F32)
        pick = jnp.where(
            jnp.logical_and(norm_row - target * 4 == lax.div(norm_target, 32), norm_fits), 1.0, 0.0
        ).astype(BF16)
        for part in norm_terms:
            total += lax.dot_general(part, pick, TN, preferred_element_type=F32)
        for i in range(4):
            gather = jnp.where(
                jnp.logical_and(
                    jnp.logical_and(same_head, delta_term), lax.div(target_lane, 32) == i
                ), 1.0, 0.0,
            ).astype(BF16)
            product = g_own[target * 4 + i].astype(F32) * o_own[target * 4 + i].astype(F32)
            high = product.astype(BF16)
            low = (product - high.astype(F32)).astype(BF16)
            total += jnp.dot(high, gather, preferred_element_type=F32)
            total += jnp.dot(low, gather, preferred_element_type=F32)
        high, middle, low = split3(-total)
        value = jnp.where(
            jnp.logical_or(term == 0, term == 3), high,
            jnp.where(jnp.logical_or(term == 1, term == 4), middle,
                      jnp.where(jnp.logical_or(term == 2, term == 5), low,
                                jnp.where(term == 6, 1.0, 0.0))),
        )
        st_out[target] = value.astype(BF16)
        return carry

    lax.fori_loop(0, 4, stats, 0)
    target = st.at[0, xl, place, :]
    stat_swaps = [
        remote(st_out.at[quad_of[o]], target, t_send.at[o], t_recv.at[o], quad_ids[o]) for o in range(3)
    ]
    stat_swaps.append(pltpu.make_async_copy(st_out.at[quad], target, t_local.at[0]))
    for copy in stat_swaps:
        copy.start()

    def start_row(i):
        for copy in swap_row(i, queries_grads):
            copy.wait()
        for copy in pass_on(0, i):
            copy.start()

    start_row(0)

    @pl.when(jnp.logical_not(alone))
    def _():
        bias_push.wait()
        for copy in spread():
            copy.start()

    start_row(1)
    start_row(2)
    start_row(3)
    for copy in stat_swaps:
        copy.wait()
    for copy in pass_stats(0):
        copy.start()

    wide_lane = iota((192, 128), 1)
    masked = mask_own[:, 0:192]
    for other in range(1, nz):
        masked = jnp.where(z == other, mask_own[:, 192 * other:192 * other + 192], masked)
    masked = jnp.where(masked == 1, 0.0, -BIG).astype(BF16)
    mask_row, mask_lane = iota((16, 128), 0), iota((16, 128), 1)

    def weights(i):
        for copy in swap_row(i, keys_values):
            copy.wait()
        keys, values = kx[i].astype(F32), vx[i].astype(F32)
        pick = jnp.where(
            jnp.logical_and(mask_row == 4 * quad + i, lax.rem(mask_lane, 8) == 6), 1.0, 0.0
        ).astype(BF16)
        mask_lanes = lax.dot_general(masked, pick, TN, preferred_element_type=F32)
        zero = jnp.zeros((192, 128), F32)
        for h in range(HEADS):
            head = lax.div(wide_lane, 32) == h
            block = pl.ds(h * 192, 192)
            offset = wide_lane - (i * 32 + h * 8)
            ws[i, block, 0:128] = jnp.where(head, keys, zero).astype(BF16)
            wp[i, block, 0:128] = jnp.where(head, values, zero).astype(BF16)
            ws[i, block, 128:256] = jnp.where(
                jnp.logical_and(offset >= 0, offset < 3), 1.0, jnp.where(offset == 6, mask_lanes, zero)
            ).astype(BF16)
            wp[i, block, 128:256] = jnp.where(
                jnp.logical_and(offset >= 3, offset < 6), 1.0, zero
            ).astype(BF16)
        dk_acc[i] = jnp.zeros(dk_acc.shape[1:], F32)
        dv_acc[i] = jnp.zeros(dv_acc.shape[1:], F32)

    def bias_core(s):
        part = bias_all.at[s, core]
        return remote(part, part, bc_send.at[s], bc_recv.at[s], core_id)

    def share_bias(s):
        for w in range(2):
            @pl.when(jnp.logical_or(s != own_step, xl != w))
            def _():
                part = bias_all.at[s, core, w]
                remote(part, part, by_send.at[0], by_recv.at[s, w], core_id).wait_recv()

        bias_core(s).start()

    share_bias(0)

    def sum_core(s):
        return remote(db_send.at[s], db_core.at[s], dc_send.at[s], dc_recv.at[s], core_id)

    def to_sum(s, w):
        owner = lax.rem(z + s, nz)
        o_x = lax.rem(lax.rem(owner, nxh) * 2 + w - x + nx, nx)
        o = lax.rem(lax.div(owner, nxh) - y + ny, ny) * nx + o_x
        at = jnp.where(o > 0, o - 1, 0)
        return o, remote(
            db_keep.at[s, w], db_owned.at[at], do_send.at[s, w], do_recv.at[at],
            {"row": owner, "col": z * 4 + w * 2 + core},
        )

    place_in_plane = row * 2 + xl

    def straight_home(s, w):
        return remote(
            db_keep.at[s, w], db_parts.at[place_in_plane], do_send.at[s, w], dp_recv.at[place_in_plane],
            home_of(s, w),
        )

    def share_sum(s):
        for w in range(2):
            rows = pl.ds(pl.multiple_of(w * 96 + (1 - core) * 48, 48), 48)
            db_send[s, w] = db_acc[s, rows, :].astype(BF16)
        sum_core(s).start()

    def add_cores(s):
        sum_core(s).wait_recv()
        for w in range(2):
            rows = pl.ds(pl.multiple_of(w * 96 + core * 48, 48), 48)
            whole = db_acc[s, rows, :] + db_core[s, w].astype(F32)
            db_acc[s, rows, :] = whole
            db_keep[s, w] = whole.astype(BF16)

        @pl.when(s < last)
        def _():
            for w in range(2):
                o, copy = to_sum(s, w)
                pl.when(o > 0)(copy.start)

        @pl.when(s >= last)
        def _():
            for w in range(2):
                straight_home(s, w).start()

    def turned(acc, i, factor):
        blocks = []
        for t in range(3):
            unit = jnp.where(iota((64, 128), 0) + 32 * t == iota((64, 128), 1), 1.0, 0.0).astype(BF16)
            part = (acc[i, t] * F32(factor)).astype(BF16)
            blocks.append(lax.dot_general(part, unit, TN, preferred_element_type=F32))
        stacked = jnp.concatenate(blocks, axis=0)
        total = jnp.zeros((192, 128), F32)
        for h in range(HEADS):
            total = jnp.where(lax.div(wide_lane, 32) == h, stacked[192 * h:192 * h + 192], total)
        return total.astype(BF16)

    outs = (dq_out, dk_out, dv_out)

    def give_back(at, i):
        copies = []
        for o in range(3):
            columns = pl.ds(pl.multiple_of(quad_of[o] * 48, 48), 48)
            copies.append(remote(
                back.at[at, i, columns, :], outs[at].at[4 * quad + i],
                e_send.at[at, i, o], e_recv.at[at, i, o], quad_ids[o],
            ))
        copies.append(pltpu.make_async_copy(back.at[at, i, mine, :], outs[at].at[4 * quad + i], e_local.at[at, i]))
        return copies

    def one_row(s, i):
        @pl.when(s == 0)
        def _():
            weights(i)

        queries = jnp.concatenate([qg[s, i, 0, 0], qg[s, i, 1, 0]], axis=0)
        grads = jnp.concatenate([qg[s, i, 0, 1], qg[s, i, 1, 1]], axis=0)
        terms = jnp.concatenate([st[s, 0], st[s, 1]], axis=0)
        left_s = jnp.concatenate([queries, terms], axis=1)
        left_p = jnp.concatenate([grads, terms], axis=1)
        queries_t, grads_t = queries.T, grads.T
        grad_query = jnp.zeros((192, 128), F32)
        for t in range(3):
            span = pl.ds(256 * t, 256)
            logits = lax.dot_general(left_s, ws[i, span, :], NT, preferred_element_type=F32)
            prob_grad = lax.dot_general(left_p, wp[i, span, :], NT, preferred_element_type=F32)
            bias = jnp.concatenate(
                [bias_all[s, c, w, :, span] for w in range(2) for c in range(2)], axis=0
            ).astype(F32)
            probs = jnp.exp(logits * F32(scaling) + bias)
            score_grad = probs * prob_grad
            probs_low = probs.astype(BF16)
            score_low = score_grad.astype(BF16)

            @pl.when(i == 0)
            def _():
                db_acc[s, :, span] = score_grad

            @pl.when(i > 0)
            def _():
                db_acc[s, :, span] += score_grad

            grad_query += jnp.dot(score_low, ws[i, span, 0:128], preferred_element_type=F32)
            part = slice(32 * t, 32 * t + 64)
            dk_acc[i, t] += jnp.dot(queries_t[part], score_low, preferred_element_type=F32)
            dv_acc[i, t] += jnp.dot(grads_t[part], probs_low, preferred_element_type=F32)

        @pl.when(s < nz - 1)
        def _():
            for copy in pass_on(s, i):
                copy.wait_recv()

            @pl.when(s < nz - 2)
            def _():
                for copy in pass_on(s + 1, i):
                    copy.start()

        @pl.when(s == 0)
        def _():
            dq_own[i] = grad_query

        @pl.when(s == 1)
        def _():
            acc_out[1, i, 0] = grad_query[:96].astype(BF16)
            acc_out[1, i, 1] = grad_query[96:].astype(BF16)

        @pl.when(s > 1)
        def _():
            for copy in pass_sum(s - 1, i):
                copy.wait_recv()
            acc_out[s, i, 0] = (grad_query[:96] + acc_in[s, i, 0].astype(F32)).astype(BF16)
            acc_out[s, i, 1] = (grad_query[96:] + acc_in[s, i, 1].astype(F32)).astype(BF16)

        @pl.when(s > 0)
        def _():
            for copy in pass_sum(s, i):
                copy.start()

        @pl.when(s == nz - 1)
        def _():
            back[1, i] = turned(dk_acc, i, scaling)
            back[2, i] = turned(dv_acc, i, 1.0)
            for at in (1, 2):
                for copy in give_back(at, i):
                    copy.start()

    def one_step(s, carry):
        bias_core(s).wait_recv()

        def rows(i, inner):
            one_row(s, i)

            @pl.when(jnp.logical_and(i == 1, s > 0))
            def _():
                add_cores(s - 1)

            @pl.when(jnp.logical_and(i == 2, s < nz - 1))
            def _():
                share_bias(s + 1)

            return inner

        lax.fori_loop(0, 4, rows, 0)
        share_sum(s)

        @pl.when(s < nz - 1)
        def _():
            for copy in pass_stats(s):
                copy.wait_recv()

            @pl.when(s < nz - 2)
            def _():
                for copy in pass_stats(s + 1):
                    copy.start()

        return carry

    lax.fori_loop(0, nz, one_step, 0)

    def finish_query(i, carry):
        for copy in pass_sum(nz - 1, i):
            copy.wait_recv()
        for w in range(2):
            part = pl.ds(96 * w, 96)
            whole = dq_own[i, part, :] + acc_in[nz, i, w].astype(F32)
            back[0, i, part, :] = (whole * F32(scaling)).astype(BF16)
        for copy in give_back(0, i):
            copy.start()
        return carry

    add_cores(nz - 1)

    home_push = remote(db_home, db_whole, dh_send.at[0], dh_recv.at[0], to_home)

    @pl.when(own_step < last)
    def _():
        whole = db_acc[own_step, pl.ds(pl.multiple_of(xl * 96 + core * 48, 48), 48), :]
        for o in range(nx * ny - 1):
            remote(db_home, db_owned.at[o], dh_send.at[0], do_recv.at[o], to_home).wait_recv()
            whole = whole + db_owned[o].astype(F32)
        db_home[...] = whole.astype(BF16)

        @pl.when(jnp.logical_not(alone))
        def _():
            home_push.start()

    lax.fori_loop(0, 4, finish_query, 0)

    def write_out(whole):
        for h in range(HEADS):
            db_final[h] = whole[:, 192 * h:192 * h + 192].astype(BF16)

    @pl.when(alone)
    def _():
        write_out(db_home[...].astype(F32))

    @pl.when(jnp.logical_and(home_step > 0, home_step < last))
    def _():
        home_push.wait_recv()
        write_out(db_whole[...].astype(F32))

    @pl.when(home_step >= last)
    def _():
        whole = jnp.zeros((48, 768), F32)
        for o in range(nx * ny):
            remote(db_home, db_parts.at[o], dh_send.at[0], dp_recv.at[o], to_home).wait_recv()
            whole = whole + db_parts[o].astype(F32)
        write_out(whole)

    final = pltpu.make_async_copy(db_final, db_out, h_local.at[0])
    final.start()

    @pl.when(jnp.logical_and(own_step < last, jnp.logical_not(alone)))
    def _():
        home_push.wait_send()

    def sent(s, carry):
        def rows(i, inner):
            @pl.when(s < nz - 1)
            def _():
                for copy in pass_on(s, i):
                    copy.wait_send()

            @pl.when(s > 0)
            def _():
                for copy in pass_sum(s, i):
                    copy.wait_send()

            return inner

        lax.fori_loop(0, 4, rows, 0)

        @pl.when(s < nz - 1)
        def _():
            for copy in pass_stats(s):
                copy.wait_send()

        bias_core(s).wait_send()
        sum_core(s).wait_send()

        for w in range(2):
            @pl.when(s < last)
            def _():
                o, copy = to_sum(s, w)
                pl.when(o > 0)(copy.wait_send)

            @pl.when(s >= last)
            def _():
                straight_home(s, w).wait_send()

        return carry

    lax.fori_loop(0, nz, sent, 0)
    for copy in spread():
        copy.wait_send()

    def returned(i, carry):
        for at in range(3):
            for copy in give_back(at, i):
                copy.wait()
        return carry

    lax.fori_loop(0, 4, returned, 0)

    final.wait()


def solution(mesh):
    rows_n, cols_n = mesh.shape["row"], mesh.shape["col"]
    nz = cols_n // 4
    nxh = 2 if rows_n >= 4 else 1
    ny = rows_n // nxh
    nx = 2 * nxh

    def shards(query_proj, key_proj, value_proj, attn_out, out_grad, log_norm, pair_mask, pair_bias):
        width = query_proj.shape[2]
        scaling = (width // HEADS) ** -0.5
        anywhere = pl.BlockSpec(memory_space=pl.ANY)
        dma = pltpu.SemaphoreType.DMA
        shapes = (
            jax.ShapeDtypeStruct((16, 48, 128), BF16),
            jax.ShapeDtypeStruct((16, 48, 128), BF16),
            jax.ShapeDtypeStruct((16, 48, 128), BF16),
            jax.ShapeDtypeStruct((HEADS, 48, 192), BF16),
        )
        results = pl.pallas_call(
            functools.partial(kernel, (ny, nxh, nz), scaling),
            out_shape=shapes,
            in_specs=[anywhere] * 8,
            out_specs=(anywhere,) * 4,
            scratch_shapes=[
                pltpu.VMEM((16, 48, 128), BF16),
                pltpu.VMEM((16, 48, 128), BF16),
                pltpu.VMEM((HEADS, 16, 48), F32),
                pltpu.VMEM((16, nz * 192), jnp.int32),
                pltpu.VMEM((HEADS, 48, 192), BF16),
                pltpu.VMEM((48, 768), BF16),
                pltpu.VMEM((nz, 4, 2, 2, 96, 128), BF16),
                pltpu.VMEM((nz, 2, 96, 128), BF16),
                pltpu.VMEM((4, 48, 128), BF16),
                pltpu.VMEM((4, 192, 128), BF16),
                pltpu.VMEM((4, 192, 128), BF16),
                pltpu.VMEM((4, 768, 256), BF16),
                pltpu.VMEM((4, 768, 256), BF16),
                pltpu.VMEM((nz, 2, 2, 48, 768), BF16),
                pltpu.VMEM((nz + 1, 4, 2, 96, 128), BF16),
                pltpu.VMEM((nz, 4, 2, 96, 128), BF16),
                pltpu.VMEM((4, 192, 128), F32),
                pltpu.VMEM((4, 3, 64, 256), F32),
                pltpu.VMEM((4, 3, 64, 256), F32),
                pltpu.VMEM((nz, 192, 768), F32),
                pltpu.VMEM((3, 4, 192, 128), BF16),
                pltpu.VMEM((nz, 2, 48, 768), BF16),
                pltpu.VMEM((nz, 2, 48, 768), BF16),
                pltpu.VMEM((nz, 2, 48, 768), BF16),
                pltpu.VMEM((nx * ny - 1, 48, 768), BF16),
                pltpu.VMEM((nx * ny, 48, 768), BF16),
                pltpu.VMEM((48, 768), BF16),
                pltpu.VMEM((48, 768), BF16),
                pltpu.VMEM((HEADS, 48, 192), BF16),
                dma((5,)),
                dma((4, 4, 3)), dma((4, 4, 3)), dma((4, 4)),
                dma((3,)), dma((3,)), dma((1,)),
                dma((nz, 4, 2)), dma((nz, 4, 2)),
                dma((nz, 2)), dma((nz, 2)),
                dma((nz, 4, 2)), dma((nz + 1, 4, 2)),
                dma((1,)), dma((1,)),
                dma((nx * ny - 1,)), dma((nz, 2)),
                dma((nz,)), dma((nz,)),
                dma((nz,)), dma((nz,)),
                dma((nz, 2)), dma((nx * ny - 1,)),
                dma((nx * ny,)),
                dma((1,)), dma((1,)),
                dma((3, 4, 3)), dma((3, 4, 3)), dma((3, 4)),
                dma((1,)),
            ],
            compiler_params=pltpu.CompilerParams(
                collective_id=0, has_side_effects=True, vmem_limit_bytes=56 * 1024 * 1024
            ),
        )(query_proj, key_proj, value_proj, attn_out, out_grad, log_norm, pair_mask, pair_bias)
        return results

    placed = (
        P("row", "col", None), P("row", "col", None), P("row", "col", None), P("row", "col", None),
        P("row", "col", None), P(None, "row", "col"), P("row", None), P(None, "col", "row"),
    )
    return jax.shard_map(
        shards,
        mesh=mesh,
        in_specs=placed,
        out_specs=(P("row", "col", None), P("row", "col", None), P("row", "col", None), P(None, "col", "row")),
        check_vma=False,
    )
```

```python
import functools

import jax
import jax.numpy as jnp
from jax import lax
from jax.experimental import pallas as pl
from jax.experimental.pallas import tpu as pltpu
from jax.sharding import PartitionSpec as P

MESH = pl.DeviceIdType.MESH
HEADS = 4
BIG = 1.0e30
F32 = jnp.float32
BF16 = jnp.bfloat16
NT = (((1,), (1,)), ((), ()))
TN = (((0,), (0,)), ((), ()))


def iota(shape, axis):
    return lax.broadcasted_iota(jnp.int32, shape, axis)


def split3(value):
    high = value.astype(BF16).astype(F32)
    rest = value - high
    middle = rest.astype(BF16).astype(F32)
    low = (rest - middle).astype(BF16).astype(F32)
    return high, middle, low


def kernel(
    geometry, scaling,
    q_ref, k_ref, v_ref, o_ref, g_ref, ln_ref, mask_ref, bias_ref,
    dq_out, dk_out, dv_out, db_out,
    o_own, g_own, ln_own, mask_own, bias_own, bias_wide,
    qg, st, st_out, kx, vx, ws, wp, bias_all,
    acc_in, acc_out, dq_own, dk_acc, dv_acc, db_acc,
    back, db_send, db_core, db_keep, db_in, db_part, db_whole, db_final,
    load, qg_send, qg_recv, qg_local, t_send, t_recv, t_local,
    r_send, r_recv, s_send, s_recv, a_send, a_recv,
    bp_send, bp_recv, by_send, by_recv, bc_send, bc_recv,
    dc_send, dc_recv, dy_send, dy_recv, dh_send, dh_recv,
    e_send, e_recv, e_local, h_local,
):
    ny, nxh, nz = geometry
    nx = 2 * nxh
    row = lax.axis_index("row")
    col = lax.axis_index("col")
    y, xh = lax.div(row, nxh), lax.rem(row, nxh)
    z, quad = lax.div(col, 4), lax.rem(col, 4)
    xl, core = lax.div(quad, 2), lax.rem(quad, 2)
    x = xh * 2 + xl
    right, left = lax.rem(z + 1, nz), lax.rem(z + nz - 1, nz)
    right_id = {"col": right * 4 + quad}
    left_id = {"col": left * 4 + quad}
    quad_of = [lax.rem(quad + o, 4) for o in range(1, 4)]
    quad_ids = [{"col": z * 4 + p} for p in quad_of]
    plane_ids = []
    for o in range(1, nx * ny):
        px, py = lax.rem(x + o % nx, nx), lax.rem(y + o // nx, ny)
        plane_ids.append({"row": py * nxh + lax.div(px, 2), "col": z * 4 + lax.rem(px, 2) * 2 + core})
    core_id = {"col": z * 4 + xl * 2 + 1 - core}
    chips = nx * ny
    deep = 16 * max(1, 12 // chips)
    owners, pieces = 192 // deep, 48 // deep
    chip = row * 2 + xl
    active = chip < owners
    own_rows = pl.ds(pl.multiple_of(jnp.where(active, chip, 0) * deep, deep), deep)
    origin = lax.div(jnp.where(active, chip, 0) * deep, 48)
    own_piece = jnp.logical_and(jnp.logical_and(row == z, active), origin == quad)
    home_step = jnp.where(xl == 0, lax.rem(row - z + nz, nz), lax.rem(z - row + nz, nz))
    owner_ids = []
    for m in range(pieces):
        for c in range(2):
            at = quad * pieces + m
            owner_ids.append((
                m, c, jnp.logical_and(own_piece, jnp.logical_and(at == chip, core == c)),
                {"row": lax.div(at, 2), "col": row * 4 + lax.rem(at, 2) * 2 + c},
            ))

    def home_of(s):
        at = jnp.where(origin < 2, z + nz - s, z + s)
        return {"row": z, "col": lax.rem(at, nz) * 4 + origin}

    loads = [
        pltpu.make_async_copy(source, target, load.at[at])
        for at, (source, target) in enumerate(
            [(bias_ref, bias_own), (g_ref, g_own), (o_ref, o_own), (ln_ref, ln_own), (mask_ref, mask_own)]
        )
    ]
    for copy in loads:
        copy.start()

    barrier = pltpu.get_barrier_semaphore()
    greeted = quad_ids + [right_id, left_id] + plane_ids
    for peer in greeted:
        pl.semaphore_signal(barrier, inc=1, device_id=peer, device_id_type=MESH)

    for _, _, same, peer in owner_ids:
        @pl.when(jnp.logical_not(same))
        def _():
            pl.semaphore_signal(barrier, inc=1, device_id=peer, device_id_type=MESH)

    for s in range(nz):
        @pl.when(jnp.logical_and(active, jnp.logical_not(jnp.logical_and(own_piece, s == 0))))
        def _():
            pl.semaphore_signal(barrier, inc=1, device_id=home_of(s), device_id_type=MESH)

    loads[0].wait()
    lanes = jnp.concatenate([bias_own[h] for h in range(HEADS)], axis=1)
    bias_wide[0] = lanes[:, :384]
    bias_wide[1] = lanes[:, 384:]

    pl.semaphore_wait(barrier,
        len(greeted) + 2 * pieces + jnp.where(active, nz, 0) - jnp.where(own_piece, 2, 0)
    )

    def remote(source, target, send, recv, device):
        return pltpu.make_async_remote_copy(
            src_ref=source, dst_ref=target, send_sem=send, recv_sem=recv,
            device_id=device, device_id_type=MESH,
        )

    place = pl.ds(pl.multiple_of(core * 48, 48), 48)
    mine = pl.ds(pl.multiple_of(quad * 48, 48), 48)

    def swap_row(i, sources):
        copies = []
        for at, source in sources:
            target = (qg.at[0, i, xl, at, place, :] if at < 2 else (kx, vx)[at - 2].at[i, mine, :])
            for o in range(3):
                copies.append(remote(
                    source.at[4 * quad_of[o] + i], target,
                    qg_send.at[at, i, o], qg_recv.at[at, i, o], quad_ids[o],
                ))
            copies.append(pltpu.make_async_copy(source.at[4 * quad + i], target, qg_local.at[at, i]))
        return copies

    queries_grads = ((0, q_ref), (1, g_ref))
    keys_values = ((2, k_ref), (3, v_ref))
    for i in range(4):
        for copy in swap_row(i, queries_grads):
            copy.start()

    def push(m, c, peer):
        rows = pl.ds(pl.multiple_of(quad * 48 + m * deep, deep), deep)
        return remote(
            bias_wide.at[c, pl.ds(m * deep, deep)], bias_all.at[home_step, c, rows],
            bp_send.at[m, c], bp_recv.at[home_step], peer,
        )

    for m, c, same, peer in owner_ids:
        @pl.when(jnp.logical_not(same))
        def _():
            push(m, c, peer).start()

        @pl.when(same)
        def _():
            bias_all[0, c, own_rows] = bias_wide[c, m * deep:(m + 1) * deep]

    for i in range(4):
        for copy in swap_row(i, keys_values):
            copy.start()

    def pass_on(s, i):
        return [
            remote(qg.at[s, i, 0], qg.at[s + 1, i, 0], r_send.at[s, i, 0], r_recv.at[s + 1, i, 0], right_id),
            remote(qg.at[s, i, 1], qg.at[s + 1, i, 1], r_send.at[s, i, 1], r_recv.at[s + 1, i, 1], left_id),
        ]

    def pass_stats(s):
        return [
            remote(st.at[s, 0], st.at[s + 1, 0], s_send.at[s, 0], s_recv.at[s + 1, 0], right_id),
            remote(st.at[s, 1], st.at[s + 1, 1], s_send.at[s, 1], s_recv.at[s + 1, 1], left_id),
        ]

    def pass_sum(s, i):
        return [
            remote(acc_out.at[s, i, 0], acc_in.at[s + 1, i, 0], a_send.at[s, i, 0], a_recv.at[s + 1, i, 0], right_id),
            remote(acc_out.at[s, i, 1], acc_in.at[s + 1, i, 1], a_send.at[s, i, 1], a_recv.at[s + 1, i, 1], left_id),
        ]

    for copy in loads[1:]:
        copy.wait()
    lane = iota((48, 128), 1)
    term = lax.rem(lane, 8)
    norm = jnp.concatenate([ln_own[h] for h in range(HEADS)], axis=0) * F32(scaling ** -1)
    norm_terms = [part.astype(BF16) for part in split3(norm)]
    source_lane, target_lane = iota((128, 128), 0), iota((128, 128), 1)
    target_term = lax.rem(target_lane, 8)
    same_head = lax.div(source_lane, 32) == lax.rem(lax.div(target_lane, 8), 4)
    delta_term = jnp.logical_and(target_term >= 3, target_term < 6)
    norm_source, norm_target = iota((64, 128), 0), iota((64, 128), 1)
    norm_row = lax.rem(norm_source, 16)
    norm_fits = jnp.logical_and(
        lax.rem(norm_target, 8) < 3, lax.div(norm_source, 16) == lax.rem(lax.div(norm_target, 8), 4)
    )

    def stats(target, carry):
        total = jnp.zeros((48, 128), F32)
        pick = jnp.where(
            jnp.logical_and(norm_row - target * 4 == lax.div(norm_target, 32), norm_fits), 1.0, 0.0
        ).astype(BF16)
        for part in norm_terms:
            total += lax.dot_general(part, pick, TN, preferred_element_type=F32)
        for i in range(4):
            gather = jnp.where(
                jnp.logical_and(
                    jnp.logical_and(same_head, delta_term), lax.div(target_lane, 32) == i
                ), 1.0, 0.0,
            ).astype(BF16)
            product = g_own[target * 4 + i].astype(F32) * o_own[target * 4 + i].astype(F32)
            high = product.astype(BF16)
            low = (product - high.astype(F32)).astype(BF16)
            total += jnp.dot(high, gather, preferred_element_type=F32)
            total += jnp.dot(low, gather, preferred_element_type=F32)
        high, middle, low = split3(-total)
        value = jnp.where(
            jnp.logical_or(term == 0, term == 3), high,
            jnp.where(jnp.logical_or(term == 1, term == 4), middle,
                      jnp.where(jnp.logical_or(term == 2, term == 5), low,
                                jnp.where(term == 6, 1.0, 0.0))),
        )
        st_out[target] = value.astype(BF16)
        return carry

    lax.fori_loop(0, 4, stats, 0)
    target = st.at[0, xl, place, :]
    stat_swaps = [
        remote(st_out.at[quad_of[o]], target, t_send.at[o], t_recv.at[o], quad_ids[o]) for o in range(3)
    ]
    stat_swaps.append(pltpu.make_async_copy(st_out.at[quad], target, t_local.at[0]))
    for copy in stat_swaps:
        copy.start()

    def start_row(i):
        for copy in swap_row(i, queries_grads):
            copy.wait()
        for copy in pass_on(0, i):
            copy.start()

    start_row(0)

    def spread(s):
        @pl.when(active)
        def _():
            part = bias_all.at[s, core, own_rows]

            @pl.when(jnp.logical_not(jnp.logical_and(own_piece, s == 0)))
            def _():
                remote(part, part, bp_send.at[0, 0], bp_recv.at[s], core_id).wait_recv()

            for peer in plane_ids:
                remote(part, part, by_send.at[s], by_recv.at[s], peer).start()

    spread(0)
    start_row(1)
    start_row(2)
    start_row(3)
    for copy in stat_swaps:
        copy.wait()
    for copy in pass_stats(0):
        copy.start()

    wide_lane = iota((192, 128), 1)
    masked = mask_own[:, 0:192]
    for other in range(1, nz):
        masked = jnp.where(z == other, mask_own[:, 192 * other:192 * other + 192], masked)
    masked = jnp.where(masked == 1, 0.0, -BIG).astype(BF16)
    mask_row, mask_lane = iota((16, 128), 0), iota((16, 128), 1)

    def weights(i):
        for copy in swap_row(i, keys_values):
            copy.wait()
        keys, values = kx[i].astype(F32), vx[i].astype(F32)
        pick = jnp.where(
            jnp.logical_and(mask_row == 4 * quad + i, lax.rem(mask_lane, 8) == 6), 1.0, 0.0
        ).astype(BF16)
        mask_lanes = lax.dot_general(masked, pick, TN, preferred_element_type=F32)
        zero = jnp.zeros((192, 128), F32)
        for h in range(HEADS):
            head = lax.div(wide_lane, 32) == h
            block = pl.ds(h * 192, 192)
            offset = wide_lane - (i * 32 + h * 8)
            ws[i, block, 0:128] = jnp.where(head, keys, zero).astype(BF16)
            wp[i, block, 0:128] = jnp.where(head, values, zero).astype(BF16)
            ws[i, block, 128:256] = jnp.where(
                jnp.logical_and(offset >= 0, offset < 3), 1.0, jnp.where(offset == 6, mask_lanes, zero)
            ).astype(BF16)
            wp[i, block, 128:256] = jnp.where(
                jnp.logical_and(offset >= 3, offset < 6), 1.0, zero
            ).astype(BF16)
        dk_acc[i] = jnp.zeros(dk_acc.shape[1:], F32)
        dv_acc[i] = jnp.zeros(dv_acc.shape[1:], F32)

    def bias_core(s):
        part = bias_all.at[s, core]
        return remote(part, part, bc_send.at[s], bc_recv.at[s], core_id)

    def share_bias(s):
        def gathered(rows):
            part = bias_all.at[s, core, pl.ds(0, rows)]
            remote(part, part, by_send.at[s], by_recv.at[s], core_id).wait_recv()

        pl.when(active)(lambda: gathered(192 - deep))
        pl.when(jnp.logical_not(active))(lambda: gathered(192))
        bias_core(s).start()

    ahead, behind = min(3, nz), min(3, nz)
    for step in range(1, ahead):
        spread(step)
    for i in range(4):
        for copy in pass_on(0, i):
            copy.wait_recv()
        if nz > 2:
            for copy in pass_on(1, i):
                copy.start()
    share_bias(0)

    def sum_core(s):
        return remote(db_send.at[s], db_core.at[s], dc_send.at[s], dc_recv.at[s], core_id)

    def to_owner(s, c):
        slot = chip - jnp.where(chip > c, 1, 0)
        return remote(
            db_keep.at[s, pl.ds(c * deep, deep)], db_in.at[s, slot], dy_send.at[s], dy_recv.at[s],
            {"row": c // 2, "col": z * 4 + (c % 2) * 2 + core},
        )

    def to_home(s):
        return remote(
            db_part.at[s], db_whole.at[pl.ds(pl.multiple_of(core * 48 + lax.rem(chip * deep, 48), deep), deep)],
            dh_send.at[s], dh_recv.at[0], home_of(s),
        )

    def share_sum(s):
        db_send[s] = db_acc[s, 1 - core].astype(BF16)
        sum_core(s).start()

    def add_cores(s):
        sum_core(s).wait_recv()
        whole = db_acc[s, core] + db_core[s].astype(F32)
        db_acc[s, core] = whole
        db_keep[s] = whole.astype(BF16)
        for c in range(owners):
            @pl.when(c != chip)
            def _():
                to_owner(s, c).start()

    def add_chips(s):
        @pl.when(active)
        def _():
            remote(db_in.at[s], db_in.at[s], dy_send.at[s], dy_recv.at[s], core_id).wait_recv()
            whole = db_acc[s, core, own_rows]
            for o in range(chips - 1):
                whole = whole + db_in[s, o].astype(F32)
            own = jnp.logical_and(own_piece, s == 0)

            @pl.when(own)
            def _():
                db_whole[pl.ds(pl.multiple_of(core * 48 + lax.rem(chip * deep, 48), deep), deep)] = whole.astype(BF16)

            @pl.when(jnp.logical_not(own))
            def _():
                db_part[s] = whole.astype(BF16)
                to_home(s).start()

    def turned(acc, i, factor):
        blocks = []
        for t in range(3):
            unit = jnp.where(iota((64, 128), 0) + 32 * t == iota((64, 128), 1), 1.0, 0.0).astype(BF16)
            part = (acc[i, t] * F32(factor)).astype(BF16)
            blocks.append(lax.dot_general(part, unit, TN, preferred_element_type=F32))
        stacked = jnp.concatenate(blocks, axis=0)
        total = jnp.zeros((192, 128), F32)
        for h in range(HEADS):
            total = jnp.where(lax.div(wide_lane, 32) == h, stacked[192 * h:192 * h + 192], total)
        return total.astype(BF16)

    outs = (dq_out, dk_out, dv_out)

    def give_back(at, i):
        copies = []
        for o in range(3):
            columns = pl.ds(pl.multiple_of(quad_of[o] * 48, 48), 48)
            copies.append(remote(
                back.at[at, i, columns, :], outs[at].at[4 * quad + i],
                e_send.at[at, i, o], e_recv.at[at, i, o], quad_ids[o],
            ))
        copies.append(pltpu.make_async_copy(back.at[at, i, mine, :], outs[at].at[4 * quad + i], e_local.at[at, i]))
        return copies

    split = (
        ((0, slice(0, 256)),), ((0, slice(256, 384)), (1, slice(0, 128))), ((1, slice(128, 384)),)
    )

    def one_row(s, i):
        @pl.when(s == 0)
        def _():
            weights(i)

        queries = jnp.concatenate([qg[s, i, 0, 0], qg[s, i, 1, 0]], axis=0)
        grads = jnp.concatenate([qg[s, i, 0, 1], qg[s, i, 1, 1]], axis=0)
        terms = jnp.concatenate([st[s, 0], st[s, 1]], axis=0)
        left_s = jnp.concatenate([queries, terms], axis=1)
        left_p = jnp.concatenate([grads, terms], axis=1)
        queries_t, grads_t = queries.T, grads.T
        grad_query = jnp.zeros((192, 128), F32)
        for t in range(3):
            span = pl.ds(256 * t, 256)
            logits = lax.dot_general(left_s, ws[i, span, :], NT, preferred_element_type=F32)
            prob_grad = lax.dot_general(left_p, wp[i, span, :], NT, preferred_element_type=F32)
            bias = jnp.concatenate([bias_all[s, c, :, part] for c, part in split[t]], axis=1).astype(F32)
            probs = jnp.exp(logits * F32(scaling) + bias)
            score_grad = probs * prob_grad
            probs_low = probs.astype(BF16)
            score_low = score_grad.astype(BF16)

            begin = 0
            for c, part in split[t]:
                width = part.stop - part.start
                share = score_grad[:, begin:begin + width]
                begin += width

                @pl.when(i == 0)
                def _():
                    db_acc[s, c, :, part] = share

                @pl.when(i > 0)
                def _():
                    db_acc[s, c, :, part] += share

            grad_query += jnp.dot(score_low, ws[i, span, 0:128], preferred_element_type=F32)
            part = slice(32 * t, 32 * t + 64)
            dk_acc[i, t] += jnp.dot(queries_t[part], score_low, preferred_element_type=F32)
            dv_acc[i, t] += jnp.dot(grads_t[part], probs_low, preferred_element_type=F32)

        @pl.when(s < nz - 2)
        def _():
            for copy in pass_on(s + 1, i):
                copy.wait_recv()

            @pl.when(s < nz - 3)
            def _():
                for copy in pass_on(s + 2, i):
                    copy.start()

        @pl.when(s == 0)
        def _():
            dq_own[i] = grad_query

        @pl.when(s == 1)
        def _():
            acc_out[1, i, 0] = grad_query[:96].astype(BF16)
            acc_out[1, i, 1] = grad_query[96:].astype(BF16)

        @pl.when(s > 1)
        def _():
            for copy in pass_sum(s - 1, i):
                copy.wait_recv()
            acc_out[s, i, 0] = (grad_query[:96] + acc_in[s, i, 0].astype(F32)).astype(BF16)
            acc_out[s, i, 1] = (grad_query[96:] + acc_in[s, i, 1].astype(F32)).astype(BF16)

        @pl.when(s > 0)
        def _():
            for copy in pass_sum(s, i):
                copy.start()

        @pl.when(s == nz - 1)
        def _():
            back[1, i] = turned(dk_acc, i, scaling)
            back[2, i] = turned(dv_acc, i, 1.0)
            for at in (1, 2):
                for copy in give_back(at, i):
                    copy.start()

    def one_step(s, carry):
        bias_core(s).wait_recv()

        def rows(i, inner):
            one_row(s, i)

            @pl.when(jnp.logical_and(i == 1, s > 0))
            def _():
                add_cores(s - 1)

            @pl.when(jnp.logical_and(i == 2, s < nz - 1))
            def _():
                share_bias(s + 1)

            @pl.when(jnp.logical_and(i == 0, s < nz - ahead))
            def _():
                spread(s + ahead)

            @pl.when(jnp.logical_and(i == 3, s >= behind))
            def _():
                add_chips(s - behind)

            return inner

        lax.fori_loop(0, 4, rows, 0)
        share_sum(s)

        @pl.when(s < nz - 1)
        def _():
            for copy in pass_stats(s):
                copy.wait_recv()

            @pl.when(s < nz - 2)
            def _():
                for copy in pass_stats(s + 1):
                    copy.start()

        return carry

    lax.fori_loop(0, nz, one_step, 0)

    def finish_query(i, carry):
        for copy in pass_sum(nz - 1, i):
            copy.wait_recv()
        for w in range(2):
            part = pl.ds(96 * w, 96)
            whole = dq_own[i, part, :] + acc_in[nz, i, w].astype(F32)
            back[0, i, part, :] = (whole * F32(scaling)).astype(BF16)
        for copy in give_back(0, i):
            copy.start()
        return carry

    add_cores(nz - 1)
    for step in range(nz - behind, nz - 1):
        add_chips(step)
    lax.fori_loop(0, 4, finish_query, 0)
    add_chips(nz - 1)

    def sent(s, carry):
        def rows(i, inner):
            @pl.when(s < nz - 1)
            def _():
                for copy in pass_on(s, i):
                    copy.wait_send()

            @pl.when(s > 0)
            def _():
                for copy in pass_sum(s, i):
                    copy.wait_send()

            return inner

        lax.fori_loop(0, 4, rows, 0)

        @pl.when(s < nz - 1)
        def _():
            for copy in pass_stats(s):
                copy.wait_send()

        bias_core(s).wait_send()
        sum_core(s).wait_send()

        @pl.when(active)
        def _():
            remote(db_in.at[s], db_in.at[s], by_send.at[s], by_recv.at[s], core_id).wait_send()
            pl.when(jnp.logical_not(jnp.logical_and(own_piece, s == 0)))(to_home(s).wait_send)

        def passed(rows):
            part = db_keep.at[s, pl.ds(0, rows)]
            remote(part, part, dy_send.at[s], dy_recv.at[s], core_id).wait_send()

        pl.when(active)(lambda: passed(192 - deep))
        pl.when(jnp.logical_not(active))(lambda: passed(192))

        return carry

    lax.fori_loop(0, nz, sent, 0)
    for m, c, same, peer in owner_ids:
        pl.when(jnp.logical_not(same))(push(m, c, peer).wait_send)

    def returned(i, carry):
        for at in range(3):
            for copy in give_back(at, i):
                copy.wait()
        return carry

    lax.fori_loop(0, 4, returned, 0)


    def arrived(rows):
        part = db_whole.at[pl.ds(0, rows)]
        remote(part, part, dh_send.at[0], dh_recv.at[0], core_id).wait_recv()

    pl.when(own_piece)(lambda: arrived(96 - deep))
    pl.when(jnp.logical_not(own_piece))(lambda: arrived(96))
    total = jnp.concatenate([db_whole[0:48], db_whole[48:96]], axis=1).astype(F32)
    for h in range(HEADS):
        db_final[h] = total[:, 192 * h:192 * h + 192].astype(BF16)
    final = pltpu.make_async_copy(db_final, db_out, h_local.at[0])
    final.start()
    final.wait()


def solution(mesh):
    rows_n, cols_n = mesh.shape["row"], mesh.shape["col"]
    nz = cols_n // 4
    nxh = 2 if rows_n >= 4 else 1
    ny = rows_n // nxh
    nx = 2 * nxh
    deep = 16 * max(1, 12 // (nx * ny))

    def shards(query_proj, key_proj, value_proj, attn_out, out_grad, log_norm, pair_mask, pair_bias):
        width = query_proj.shape[2]
        scaling = (width // HEADS) ** -0.5
        anywhere = pl.BlockSpec(memory_space=pl.ANY)
        dma = pltpu.SemaphoreType.DMA
        shapes = (
            jax.ShapeDtypeStruct((16, 48, 128), BF16),
            jax.ShapeDtypeStruct((16, 48, 128), BF16),
            jax.ShapeDtypeStruct((16, 48, 128), BF16),
            jax.ShapeDtypeStruct((HEADS, 48, 192), BF16),
        )
        results = pl.pallas_call(
            functools.partial(kernel, (ny, nxh, nz), scaling),
            out_shape=shapes,
            in_specs=[anywhere] * 8,
            out_specs=(anywhere,) * 4,
            scratch_shapes=[
                pltpu.VMEM((16, 48, 128), BF16),
                pltpu.VMEM((16, 48, 128), BF16),
                pltpu.VMEM((HEADS, 16, 48), F32),
                pltpu.VMEM((16, nz * 192), jnp.int32),
                pltpu.VMEM((HEADS, 48, 192), BF16),
                pltpu.VMEM((2, 48, 384), BF16),
                pltpu.VMEM((nz, 4, 2, 2, 96, 128), BF16),
                pltpu.VMEM((nz, 2, 96, 128), BF16),
                pltpu.VMEM((4, 48, 128), BF16),
                pltpu.VMEM((4, 192, 128), BF16),
                pltpu.VMEM((4, 192, 128), BF16),
                pltpu.VMEM((4, 768, 256), BF16),
                pltpu.VMEM((4, 768, 256), BF16),
                pltpu.VMEM((nz, 2, 192, 384), BF16),
                pltpu.VMEM((nz + 1, 4, 2, 96, 128), BF16),
                pltpu.VMEM((nz, 4, 2, 96, 128), BF16),
                pltpu.VMEM((4, 192, 128), F32),
                pltpu.VMEM((4, 3, 64, 256), F32),
                pltpu.VMEM((4, 3, 64, 256), F32),
                pltpu.VMEM((nz, 2, 192, 384), F32),
                pltpu.VMEM((3, 4, 192, 128), BF16),
                pltpu.VMEM((nz, 192, 384), BF16),
                pltpu.VMEM((nz, 192, 384), BF16),
                pltpu.VMEM((nz, 192, 384), BF16),
                pltpu.VMEM((nz, nx * ny - 1, deep, 384), BF16),
                pltpu.VMEM((nz, deep, 384), BF16),
                pltpu.VMEM((96, 384), BF16),
                pltpu.VMEM((HEADS, 48, 192), BF16),
                dma((5,)),
                dma((4, 4, 3)), dma((4, 4, 3)), dma((4, 4)),
                dma((3,)), dma((3,)), dma((1,)),
                dma((nz, 4, 2)), dma((nz, 4, 2)),
                dma((nz, 2)), dma((nz, 2)),
                dma((nz, 4, 2)), dma((nz + 1, 4, 2)),
                dma((48 // deep, 2)), dma((nz,)),
                dma((nz,)), dma((nz,)),
                dma((nz,)), dma((nz,)),
                dma((nz,)), dma((nz,)),
                dma((nz,)), dma((nz,)),
                dma((nz,)), dma((1,)),
                dma((3, 4, 3)), dma((3, 4, 3)), dma((3, 4)),
                dma((1,)),
            ],
            compiler_params=pltpu.CompilerParams(
                collective_id=0, has_side_effects=True, vmem_limit_bytes=56 * 1024 * 1024
            ),
        )(query_proj, key_proj, value_proj, attn_out, out_grad, log_norm, pair_mask, pair_bias)
        return results

    placed = (
        P("row", "col", None), P("row", "col", None), P("row", "col", None), P("row", "col", None),
        P("row", "col", None), P(None, "row", "col"), P("row", None), P(None, "col", "row"),
    )
    return jax.shard_map(
        shards,
        mesh=mesh,
        in_specs=placed,
        out_specs=(P("row", "col", None), P("row", "col", None), P("row", "col", None), P(None, "col", "row")),
        check_vma=False,
    )
```

```python
import functools

import jax
import jax.numpy as jnp
from jax import lax
from jax.experimental import pallas as pl
from jax.experimental.pallas import tpu as pltpu
from jax.sharding import PartitionSpec as P

MESH = pl.DeviceIdType.MESH
HEADS = 4
BIG = 1.0e30
F32 = jnp.float32
BF16 = jnp.bfloat16
NT = (((1,), (1,)), ((), ()))
TN = (((0,), (0,)), ((), ()))


def iota(shape, axis):
    return lax.broadcasted_iota(jnp.int32, shape, axis)


def split3(value):
    high = value.astype(BF16).astype(F32)
    rest = value - high
    middle = rest.astype(BF16).astype(F32)
    low = (rest - middle).astype(BF16).astype(F32)
    return high, middle, low


def kernel(
    geometry, scaling,
    q_ref, k_ref, v_ref, o_ref, g_ref, ln_ref, mask_ref, bias_ref,
    dq_out, dk_out, dv_out, db_out,
    o_own, g_own, ln_own, mask_own, bias_own, bias_wide,
    qg, st, st_out, kx, vx, ws, wp, bias_all,
    acc_in, acc_out, dq_own, dk_acc, dv_acc, db_acc,
    back, db_send, db_core, db_keep, db_in, db_part, db_whole, db_final,
    load, qg_send, qg_recv, qg_local, t_send, t_recv, t_local,
    r_send, r_recv, s_send, s_recv, a_send, a_recv,
    bp_send, bp_recv, by_send, by_recv, bc_send, bc_recv,
    dc_send, dc_recv, dy_send, dy_recv, dh_send, dh_recv,
    e_send, e_recv, e_local, h_local,
):
    ny, nxh, nz = geometry
    nx = 2 * nxh
    row = lax.axis_index("row")
    col = lax.axis_index("col")
    y, xh = lax.div(row, nxh), lax.rem(row, nxh)
    z, quad = lax.div(col, 4), lax.rem(col, 4)
    xl, core = lax.div(quad, 2), lax.rem(quad, 2)
    x = xh * 2 + xl
    right, left = lax.rem(z + 1, nz), lax.rem(z + nz - 1, nz)
    right_id = {"col": right * 4 + quad}
    left_id = {"col": left * 4 + quad}
    quad_of = [lax.rem(quad + o, 4) for o in range(1, 4)]
    quad_ids = [{"col": z * 4 + p} for p in quad_of]
    plane_ids = []
    for o in range(1, nx * ny):
        px, py = lax.rem(x + o % nx, nx), lax.rem(y + o // nx, ny)
        plane_ids.append({"row": py * nxh + lax.div(px, 2), "col": z * 4 + lax.rem(px, 2) * 2 + core})
    core_id = {"col": z * 4 + xl * 2 + 1 - core}
    chips = nx * ny
    deep = 16 * max(1, 12 // chips)
    owners, pieces = 192 // deep, 48 // deep
    chip = row * 2 + xl
    active = chip < owners
    own_rows = pl.ds(pl.multiple_of(jnp.where(active, chip, 0) * deep, deep), deep)
    origin = lax.div(jnp.where(active, chip, 0) * deep, 48)
    own_piece = jnp.logical_and(jnp.logical_and(row == z, active), origin == quad)
    home_step = jnp.where(xl == 0, lax.rem(row - z + nz, nz), lax.rem(z - row + nz, nz))
    owner_ids = []
    for m in range(pieces):
        for c in range(2):
            at = quad * pieces + m
            owner_ids.append((
                m, c, jnp.logical_and(own_piece, jnp.logical_and(at == chip, core == c)),
                {"row": lax.div(at, 2), "col": row * 4 + lax.rem(at, 2) * 2 + c},
            ))

    def home_of(s):
        at = jnp.where(origin < 2, z + nz - s, z + s)
        return {"row": z, "col": lax.rem(at, nz) * 4 + origin}

    loads = [
        pltpu.make_async_copy(source, target, load.at[at])
        for at, (source, target) in enumerate(
            [(bias_ref, bias_own), (g_ref, g_own), (o_ref, o_own), (ln_ref, ln_own), (mask_ref, mask_own)]
        )
    ]
    for copy in loads:
        copy.start()

    barrier = pltpu.get_barrier_semaphore()
    greeted = quad_ids + [right_id, left_id] + plane_ids
    for peer in greeted:
        pl.semaphore_signal(barrier, inc=1, device_id=peer, device_id_type=MESH)

    for _, _, same, peer in owner_ids:
        @pl.when(jnp.logical_not(same))
        def _():
            pl.semaphore_signal(barrier, inc=1, device_id=peer, device_id_type=MESH)

    for s in range(nz):
        @pl.when(jnp.logical_and(active, jnp.logical_not(jnp.logical_and(own_piece, s == 0))))
        def _():
            pl.semaphore_signal(barrier, inc=1, device_id=home_of(s), device_id_type=MESH)

    loads[0].wait()
    lanes = jnp.concatenate([bias_own[h] for h in range(HEADS)], axis=1)
    bias_wide[0] = lanes[:, :384]
    bias_wide[1] = lanes[:, 384:]

    for copy in loads[1:]:
        copy.wait()
    lane = iota((48, 128), 1)
    term = lax.rem(lane, 8)
    norm = jnp.concatenate([ln_own[h] for h in range(HEADS)], axis=0) * F32(scaling ** -1)
    norm_terms = [part.astype(BF16) for part in split3(norm)]
    source_lane, target_lane = iota((128, 128), 0), iota((128, 128), 1)
    target_term = lax.rem(target_lane, 8)
    same_head = lax.div(source_lane, 32) == lax.rem(lax.div(target_lane, 8), 4)
    delta_term = jnp.logical_and(target_term >= 3, target_term < 6)
    norm_source, norm_target = iota((64, 128), 0), iota((64, 128), 1)
    norm_row = lax.rem(norm_source, 16)
    norm_fits = jnp.logical_and(
        lax.rem(norm_target, 8) < 3, lax.div(norm_source, 16) == lax.rem(lax.div(norm_target, 8), 4)
    )

    def stats(target, carry):
        total = jnp.zeros((48, 128), F32)
        pick = jnp.where(
            jnp.logical_and(norm_row - target * 4 == lax.div(norm_target, 32), norm_fits), 1.0, 0.0
        ).astype(BF16)
        for part in norm_terms:
            total += lax.dot_general(part, pick, TN, preferred_element_type=F32)
        for i in range(4):
            gather = jnp.where(
                jnp.logical_and(
                    jnp.logical_and(same_head, delta_term), lax.div(target_lane, 32) == i
                ), 1.0, 0.0,
            ).astype(BF16)
            product = g_own[target * 4 + i].astype(F32) * o_own[target * 4 + i].astype(F32)
            high = product.astype(BF16)
            low = (product - high.astype(F32)).astype(BF16)
            total += jnp.dot(high, gather, preferred_element_type=F32)
            total += jnp.dot(low, gather, preferred_element_type=F32)
        high, middle, low = split3(-total)
        value = jnp.where(
            jnp.logical_or(term == 0, term == 3), high,
            jnp.where(jnp.logical_or(term == 1, term == 4), middle,
                      jnp.where(jnp.logical_or(term == 2, term == 5), low,
                                jnp.where(term == 6, 1.0, 0.0))),
        )
        st_out[target] = value.astype(BF16)
        return carry

    lax.fori_loop(0, 4, stats, 0)
    pl.semaphore_wait(barrier,
        len(greeted) + 2 * pieces + jnp.where(active, nz, 0) - jnp.where(own_piece, 2, 0)
    )

    def remote(source, target, send, recv, device):
        return pltpu.make_async_remote_copy(
            src_ref=source, dst_ref=target, send_sem=send, recv_sem=recv,
            device_id=device, device_id_type=MESH,
        )

    place = pl.ds(pl.multiple_of(core * 48, 48), 48)
    mine = pl.ds(pl.multiple_of(quad * 48, 48), 48)

    def swap_row(i, sources):
        kind = 0 if sources is queries_grads else 1
        copies = []
        for at, source in sources:
            target = (qg.at[0, i, xl, at, place, :] if at < 2 else (kx, vx)[at - 2].at[i, mine, :])
            for o in range(3):
                copies.append(remote(
                    source.at[4 * quad_of[o] + i], target,
                    qg_send.at[kind], qg_recv.at[kind, i], quad_ids[o],
                ))
            copies.append(pltpu.make_async_copy(source.at[4 * quad + i], target, qg_local.at[kind, i]))
        return copies

    def swapped(i, kind):
        part = g_own.at[pl.ds(0, 6)]
        remote(part, part, qg_send.at[kind], qg_recv.at[kind, i], core_id).wait_recv()
        part = g_own.at[pl.ds(0, 2)]
        pltpu.make_async_copy(part, part, qg_local.at[kind, i]).wait()

    queries_grads = ((0, q_ref), (1, g_ref))
    keys_values = ((2, k_ref), (3, v_ref))
    for i in range(4):
        for copy in swap_row(i, queries_grads):
            copy.start()

    def push(m, c, peer):
        rows = pl.ds(pl.multiple_of(quad * 48 + m * deep, deep), deep)
        return remote(
            bias_wide.at[c, pl.ds(m * deep, deep)], bias_all.at[home_step, c, rows],
            bp_send.at[m, c], bp_recv.at[home_step], peer,
        )

    for m, c, same, peer in owner_ids:
        @pl.when(jnp.logical_not(same))
        def _():
            push(m, c, peer).start()

        @pl.when(same)
        def _():
            bias_all[0, c, own_rows] = bias_wide[c, m * deep:(m + 1) * deep]

    for i in range(4):
        for copy in swap_row(i, keys_values):
            copy.start()

    def all_of(part, send, recv):
        return remote(part, part, send, recv, core_id)

    def pass_on(s, i):
        return [
            remote(qg.at[s, i, 0], qg.at[s + 1, i, 0], r_send.at[s], r_recv.at[s + 1, i], right_id),
            remote(qg.at[s, i, 1], qg.at[s + 1, i, 1], r_send.at[s], r_recv.at[s + 1, i], left_id),
        ]

    def passed_on(s, i):
        return all_of(qg.at[s + 1, i], r_send.at[s], r_recv.at[s + 1, i])

    def pass_stats(s):
        return [
            remote(st.at[s, 0], st.at[s + 1, 0], s_send.at[s], s_recv.at[s + 1], right_id),
            remote(st.at[s, 1], st.at[s + 1, 1], s_send.at[s], s_recv.at[s + 1], left_id),
        ]

    def passed_stats(s):
        return all_of(st.at[s + 1], s_send.at[s], s_recv.at[s + 1])

    def pass_sum(s, i):
        return [
            remote(acc_out.at[s, i, 0], acc_in.at[s + 1, i, 0], a_send.at[s], a_recv.at[s + 1, i], right_id),
            remote(acc_out.at[s, i, 1], acc_in.at[s + 1, i, 1], a_send.at[s], a_recv.at[s + 1, i], left_id),
        ]

    def passed_sum(s, i):
        return all_of(acc_in.at[s + 1, i], a_send.at[s], a_recv.at[s + 1, i])

    target = st.at[0, xl, place, :]
    stat_swaps = [
        remote(st_out.at[quad_of[o]], target, t_send.at[o], t_recv.at[o], quad_ids[o]) for o in range(3)
    ]
    stat_swaps.append(pltpu.make_async_copy(st_out.at[quad], target, t_local.at[0]))
    for copy in stat_swaps:
        copy.start()

    def start_row(i):
        swapped(i, 0)
        for copy in pass_on(0, i):
            copy.start()

    start_row(0)

    def spread(s):
        @pl.when(active)
        def _():
            part = bias_all.at[s, core, own_rows]

            @pl.when(jnp.logical_not(jnp.logical_and(own_piece, s == 0)))
            def _():
                remote(part, part, bp_send.at[0, 0], bp_recv.at[s], core_id).wait_recv()

            for peer in plane_ids:
                remote(part, part, by_send.at[s], by_recv.at[s], peer).start()

    spread(0)
    start_row(1)
    start_row(2)
    start_row(3)
    for copy in stat_swaps:
        copy.wait()
    for copy in pass_stats(0):
        copy.start()

    wide_lane = iota((192, 128), 1)
    masked = mask_own[:, 0:192]
    for other in range(1, nz):
        masked = jnp.where(z == other, mask_own[:, 192 * other:192 * other + 192], masked)
    masked = jnp.where(masked == 1, 0.0, -BIG).astype(BF16)
    mask_row, mask_lane = iota((16, 128), 0), iota((16, 128), 1)

    def weights(i):
        swapped(i, 1)
        keys, values = kx[i].astype(F32), vx[i].astype(F32)
        pick = jnp.where(
            jnp.logical_and(mask_row == 4 * quad + i, lax.rem(mask_lane, 8) == 6), 1.0, 0.0
        ).astype(BF16)
        mask_lanes = lax.dot_general(masked, pick, TN, preferred_element_type=F32)
        zero = jnp.zeros((192, 128), F32)
        for h in range(HEADS):
            head = lax.div(wide_lane, 32) == h
            block = pl.ds(h * 192, 192)
            offset = wide_lane - (i * 32 + h * 8)
            ws[i, block, 0:128] = jnp.where(head, keys, zero).astype(BF16)
            wp[i, block, 0:128] = jnp.where(head, values, zero).astype(BF16)
            ws[i, block, 128:256] = jnp.where(
                jnp.logical_and(offset >= 0, offset < 3), 1.0, jnp.where(offset == 6, mask_lanes, zero)
            ).astype(BF16)
            wp[i, block, 128:256] = jnp.where(
                jnp.logical_and(offset >= 3, offset < 6), 1.0, zero
            ).astype(BF16)
        dk_acc[i] = jnp.zeros(dk_acc.shape[1:], F32)
        dv_acc[i] = jnp.zeros(dv_acc.shape[1:], F32)

    def bias_core(s):
        part = bias_all.at[s, core]
        return remote(part, part, bc_send.at[s], bc_recv.at[s], core_id)

    def share_bias(s):
        def gathered(rows):
            part = bias_all.at[s, core, pl.ds(0, rows)]
            remote(part, part, by_send.at[s], by_recv.at[s], core_id).wait_recv()

        pl.when(active)(lambda: gathered(192 - deep))
        pl.when(jnp.logical_not(active))(lambda: gathered(192))
        bias_core(s).start()

    ahead, behind = min(3, nz), min(3, nz)
    for step in range(1, ahead):
        spread(step)
    for i in range(4):
        passed_on(0, i).wait_recv()
        if nz > 2:
            for copy in pass_on(1, i):
                copy.start()
    share_bias(0)

    def sum_core(s):
        return remote(db_send.at[s], db_core.at[s], dc_send.at[s], dc_recv.at[s], core_id)

    def to_owner(s, c):
        slot = chip - jnp.where(chip > c, 1, 0)
        return remote(
            db_keep.at[s, pl.ds(c * deep, deep)], db_in.at[s, slot], dy_send.at[s], dy_recv.at[s],
            {"row": c // 2, "col": z * 4 + (c % 2) * 2 + core},
        )

    def to_home(s):
        return remote(
            db_part.at[s], db_whole.at[pl.ds(pl.multiple_of(core * 48 + lax.rem(chip * deep, 48), deep), deep)],
            dh_send.at[s], dh_recv.at[0], home_of(s),
        )

    def share_sum(s):
        db_send[s] = db_acc[s, 1 - core].astype(BF16)
        sum_core(s).start()

    def add_cores(s):
        sum_core(s).wait_recv()
        whole = db_acc[s, core] + db_core[s].astype(F32)
        db_acc[s, core] = whole
        db_keep[s] = whole.astype(BF16)
        for c in range(owners):
            @pl.when(c != chip)
            def _():
                to_owner(s, c).start()

    def add_chips(s):
        @pl.when(active)
        def _():
            remote(db_in.at[s], db_in.at[s], dy_send.at[s], dy_recv.at[s], core_id).wait_recv()
            whole = db_acc[s, core, own_rows]
            for o in range(chips - 1):
                whole = whole + db_in[s, o].astype(F32)
            own = jnp.logical_and(own_piece, s == 0)

            @pl.when(own)
            def _():
                db_whole[pl.ds(pl.multiple_of(core * 48 + lax.rem(chip * deep, 48), deep), deep)] = whole.astype(BF16)

            @pl.when(jnp.logical_not(own))
            def _():
                db_part[s] = whole.astype(BF16)
                to_home(s).start()

    def turned(acc, i, factor):
        blocks = []
        for t in range(3):
            unit = jnp.where(iota((64, 128), 0) + 32 * t == iota((64, 128), 1), 1.0, 0.0).astype(BF16)
            part = (acc[i, t] * F32(factor)).astype(BF16)
            blocks.append(lax.dot_general(part, unit, TN, preferred_element_type=F32))
        stacked = jnp.concatenate(blocks, axis=0)
        total = jnp.zeros((192, 128), F32)
        for h in range(HEADS):
            total = jnp.where(lax.div(wide_lane, 32) == h, stacked[192 * h:192 * h + 192], total)
        return total.astype(BF16)

    outs = (dq_out, dk_out, dv_out)

    def give_back(at, i):
        copies = []
        for o in range(3):
            columns = pl.ds(pl.multiple_of(quad_of[o] * 48, 48), 48)
            copies.append(remote(
                back.at[at, i, columns, :], outs[at].at[4 * quad + i],
                e_send.at[at], e_recv.at[at], quad_ids[o],
            ))
        copies.append(pltpu.make_async_copy(back.at[at, i, mine, :], outs[at].at[4 * quad + i], e_local.at[at]))
        return copies

    split = (
        ((0, slice(0, 256)),), ((0, slice(256, 384)), (1, slice(0, 128))), ((1, slice(128, 384)),)
    )

    def one_row(s, i):
        @pl.when(s == 0)
        def _():
            weights(i)

        queries = jnp.concatenate([qg[s, i, 0, 0], qg[s, i, 1, 0]], axis=0)
        grads = jnp.concatenate([qg[s, i, 0, 1], qg[s, i, 1, 1]], axis=0)
        terms = jnp.concatenate([st[s, 0], st[s, 1]], axis=0)
        left_s = jnp.concatenate([queries, terms], axis=1)
        left_p = jnp.concatenate([grads, terms], axis=1)
        queries_t, grads_t = queries.T, grads.T
        grad_query = jnp.zeros((192, 128), F32)
        for t in range(3):
            span = pl.ds(256 * t, 256)
            logits = lax.dot_general(left_s, ws[i, span, :], NT, preferred_element_type=F32)
            prob_grad = lax.dot_general(left_p, wp[i, span, :], NT, preferred_element_type=F32)
            bias = jnp.concatenate([bias_all[s, c, :, part] for c, part in split[t]], axis=1).astype(F32)
            probs = jnp.exp(logits * F32(scaling) + bias)
            score_grad = probs * prob_grad
            probs_low = probs.astype(BF16)
            score_low = score_grad.astype(BF16)

            begin = 0
            for c, part in split[t]:
                width = part.stop - part.start
                share = score_grad[:, begin:begin + width]
                begin += width

                @pl.when(i == 0)
                def _():
                    db_acc[s, c, :, part] = share

                @pl.when(i > 0)
                def _():
                    db_acc[s, c, :, part] += share

            grad_query += jnp.dot(score_low, ws[i, span, 0:128], preferred_element_type=F32)
            part = slice(32 * t, 32 * t + 64)
            dk_acc[i, t] += jnp.dot(queries_t[part], score_low, preferred_element_type=F32)
            dv_acc[i, t] += jnp.dot(grads_t[part], probs_low, preferred_element_type=F32)

        @pl.when(s < nz - 2)
        def _():
            passed_on(s + 1, i).wait_recv()

            @pl.when(s < nz - 3)
            def _():
                for copy in pass_on(s + 2, i):
                    copy.start()

        @pl.when(s == 0)
        def _():
            dq_own[i] = grad_query

        @pl.when(s == 1)
        def _():
            acc_out[1, i, 0] = grad_query[:96].astype(BF16)
            acc_out[1, i, 1] = grad_query[96:].astype(BF16)

        @pl.when(s > 1)
        def _():
            passed_sum(s - 1, i).wait_recv()
            acc_out[s, i, 0] = (grad_query[:96] + acc_in[s, i, 0].astype(F32)).astype(BF16)
            acc_out[s, i, 1] = (grad_query[96:] + acc_in[s, i, 1].astype(F32)).astype(BF16)

        @pl.when(s > 0)
        def _():
            for copy in pass_sum(s, i):
                copy.start()

        @pl.when(s == nz - 1)
        def _():
            back[1, i] = turned(dk_acc, i, scaling)
            back[2, i] = turned(dv_acc, i, 1.0)
            for at in (1, 2):
                for copy in give_back(at, i):
                    copy.start()

    def one_step(s, carry):
        bias_core(s).wait_recv()

        def rows(i, inner):
            one_row(s, i)

            @pl.when(jnp.logical_and(i == 1, s > 0))
            def _():
                add_cores(s - 1)

            @pl.when(jnp.logical_and(i == 2, s < nz - 1))
            def _():
                share_bias(s + 1)

            @pl.when(jnp.logical_and(i == 0, s < nz - ahead))
            def _():
                spread(s + ahead)

            @pl.when(jnp.logical_and(i == 3, s >= behind))
            def _():
                add_chips(s - behind)

            return inner

        lax.fori_loop(0, 4, rows, 0)
        share_sum(s)

        @pl.when(s < nz - 1)
        def _():
            passed_stats(s).wait_recv()

            @pl.when(s < nz - 2)
            def _():
                for copy in pass_stats(s + 1):
                    copy.start()

        return carry

    lax.fori_loop(0, nz, one_step, 0)

    def finish_query(i, carry):
        passed_sum(nz - 1, i).wait_recv()
        for w in range(2):
            part = pl.ds(96 * w, 96)
            whole = dq_own[i, part, :] + acc_in[nz, i, w].astype(F32)
            back[0, i, part, :] = (whole * F32(scaling)).astype(BF16)
        for copy in give_back(0, i):
            copy.start()
        return carry

    add_cores(nz - 1)
    for step in range(nz - behind, nz - 1):
        add_chips(step)
    lax.fori_loop(0, 4, finish_query, 0)
    add_chips(nz - 1)

    def sent(s, carry):
        @pl.when(s < nz - 1)
        def _():
            all_of(qg.at[s], r_send.at[s], r_recv.at[s, 0]).wait_send()
            passed_stats(s).wait_send()

        @pl.when(s > 0)
        def _():
            all_of(acc_out.at[s], a_send.at[s], a_recv.at[s, 0]).wait_send()

        bias_core(s).wait_send()
        sum_core(s).wait_send()

        @pl.when(active)
        def _():
            remote(db_in.at[s], db_in.at[s], by_send.at[s], by_recv.at[s], core_id).wait_send()
            pl.when(jnp.logical_not(jnp.logical_and(own_piece, s == 0)))(to_home(s).wait_send)

        def passed(rows):
            part = db_keep.at[s, pl.ds(0, rows)]
            remote(part, part, dy_send.at[s], dy_recv.at[s], core_id).wait_send()

        pl.when(active)(lambda: passed(192 - deep))
        pl.when(jnp.logical_not(active))(lambda: passed(192))

        return carry

    lax.fori_loop(0, nz, sent, 0)
    for m, c, same, peer in owner_ids:
        pl.when(jnp.logical_not(same))(push(m, c, peer).wait_send)

    for kind in range(2):
        all_of(g_own.at[pl.ds(0, 12)], qg_send.at[kind], qg_recv.at[kind, 0]).wait_send()
        all_of(g_own.at[pl.ds(0, 12)], qg_send.at[kind], qg_recv.at[kind, 0]).wait_send()
    for at in range(3):
        all_of(back.at[at, pl.ds(0, 3)], e_send.at[at], e_recv.at[at]).wait()
        pltpu.make_async_copy(back.at[at, 0], back.at[at, 0], e_local.at[at]).wait()

    def arrived(rows):
        part = db_whole.at[pl.ds(0, rows)]
        remote(part, part, dh_send.at[0], dh_recv.at[0], core_id).wait_recv()

    pl.when(own_piece)(lambda: arrived(96 - deep))
    pl.when(jnp.logical_not(own_piece))(lambda: arrived(96))
    total = jnp.concatenate([db_whole[0:48], db_whole[48:96]], axis=1).astype(F32)
    for h in range(HEADS):
        db_final[h] = total[:, 192 * h:192 * h + 192].astype(BF16)
    final = pltpu.make_async_copy(db_final, db_out, h_local.at[0])
    final.start()
    final.wait()


def solution(mesh):
    rows_n, cols_n = mesh.shape["row"], mesh.shape["col"]
    nz = cols_n // 4
    nxh = 2 if rows_n >= 4 else 1
    ny = rows_n // nxh
    nx = 2 * nxh
    deep = 16 * max(1, 12 // (nx * ny))

    def shards(query_proj, key_proj, value_proj, attn_out, out_grad, log_norm, pair_mask, pair_bias):
        width = query_proj.shape[2]
        scaling = (width // HEADS) ** -0.5
        anywhere = pl.BlockSpec(memory_space=pl.ANY)
        dma = pltpu.SemaphoreType.DMA
        shapes = (
            jax.ShapeDtypeStruct((16, 48, 128), BF16),
            jax.ShapeDtypeStruct((16, 48, 128), BF16),
            jax.ShapeDtypeStruct((16, 48, 128), BF16),
            jax.ShapeDtypeStruct((HEADS, 48, 192), BF16),
        )
        results = pl.pallas_call(
            functools.partial(kernel, (ny, nxh, nz), scaling),
            out_shape=shapes,
            in_specs=[anywhere] * 8,
            out_specs=(anywhere,) * 4,
            scratch_shapes=[
                pltpu.VMEM((16, 48, 128), BF16),
                pltpu.VMEM((16, 48, 128), BF16),
                pltpu.VMEM((HEADS, 16, 48), F32),
                pltpu.VMEM((16, nz * 192), jnp.int32),
                pltpu.VMEM((HEADS, 48, 192), BF16),
                pltpu.VMEM((2, 48, 384), BF16),
                pltpu.VMEM((nz, 4, 2, 2, 96, 128), BF16),
                pltpu.VMEM((nz, 2, 96, 128), BF16),
                pltpu.VMEM((4, 48, 128), BF16),
                pltpu.VMEM((4, 192, 128), BF16),
                pltpu.VMEM((4, 192, 128), BF16),
                pltpu.VMEM((4, 768, 256), BF16),
                pltpu.VMEM((4, 768, 256), BF16),
                pltpu.VMEM((nz, 2, 192, 384), BF16),
                pltpu.VMEM((nz + 1, 4, 2, 96, 128), BF16),
                pltpu.VMEM((nz, 4, 2, 96, 128), BF16),
                pltpu.VMEM((4, 192, 128), F32),
                pltpu.VMEM((4, 3, 64, 256), F32),
                pltpu.VMEM((4, 3, 64, 256), F32),
                pltpu.VMEM((nz, 2, 192, 384), F32),
                pltpu.VMEM((3, 4, 192, 128), BF16),
                pltpu.VMEM((nz, 192, 384), BF16),
                pltpu.VMEM((nz, 192, 384), BF16),
                pltpu.VMEM((nz, 192, 384), BF16),
                pltpu.VMEM((nz, nx * ny - 1, deep, 384), BF16),
                pltpu.VMEM((nz, deep, 384), BF16),
                pltpu.VMEM((96, 384), BF16),
                pltpu.VMEM((HEADS, 48, 192), BF16),
                dma((5,)),
                dma((2,)), dma((2, 4)), dma((2, 4)),
                dma((3,)), dma((3,)), dma((1,)),
                dma((nz,)), dma((nz, 4)),
                dma((nz,)), dma((nz,)),
                dma((nz,)), dma((nz + 1, 4)),
                dma((48 // deep, 2)), dma((nz,)),
                dma((nz,)), dma((nz,)),
                dma((nz,)), dma((nz,)),
                dma((nz,)), dma((nz,)),
                dma((nz,)), dma((nz,)),
                dma((nz,)), dma((1,)),
                dma((3,)), dma((3,)), dma((3,)),
                dma((1,)),
            ],
            compiler_params=pltpu.CompilerParams(
                collective_id=0, has_side_effects=True, vmem_limit_bytes=56 * 1024 * 1024
            ),
        )(query_proj, key_proj, value_proj, attn_out, out_grad, log_norm, pair_mask, pair_bias)
        return results

    placed = (
        P("row", "col", None), P("row", "col", None), P("row", "col", None), P("row", "col", None),
        P("row", "col", None), P(None, "row", "col"), P("row", None), P(None, "col", "row"),
    )
    return jax.shard_map(
        shards,
        mesh=mesh,
        in_specs=placed,
        out_specs=(P("row", "col", None), P("row", "col", None), P("row", "col", None), P(None, "col", "row")),
        check_vma=False,
    )
```

```python
import functools

import jax
import jax.numpy as jnp
from jax import lax
from jax.experimental import pallas as pl
from jax.experimental.pallas import tpu as pltpu
from jax.sharding import PartitionSpec as P

MESH = pl.DeviceIdType.MESH
HEADS = 4
BIG = 1.0e30
F32 = jnp.float32
BF16 = jnp.bfloat16
NT = (((1,), (1,)), ((), ()))
TN = (((0,), (0,)), ((), ()))


def iota(shape, axis):
    return lax.broadcasted_iota(jnp.int32, shape, axis)


def split3(value):
    high = value.astype(BF16).astype(F32)
    rest = value - high
    middle = rest.astype(BF16).astype(F32)
    low = (rest - middle).astype(BF16).astype(F32)
    return high, middle, low


def kernel(
    geometry, scaling,
    q_ref, k_ref, v_ref, o_ref, g_ref, ln_ref, mask_ref, bias_ref,
    dq_out, dk_out, dv_out, db_out,
    o_own, g_own, ln_own, mask_own, bias_own, bias_wide,
    qg, st, st_out, kx, vx, ws, wp, ws_t, wp_t, bias_all,
    acc_in, acc_out, dq_own, dk_acc, dv_acc, db_acc,
    back, db_send, db_core, db_keep, db_in, db_part, db_whole, db_final,
    load, qg_send, qg_recv, qg_local, t_send, t_recv, t_local,
    r_send, r_recv, s_send, s_recv, a_send, a_recv,
    bp_send, bp_recv, by_send, by_recv, bc_send, bc_recv,
    dc_send, dc_recv, dy_send, dy_recv, dh_send, dh_recv,
    e_send, e_recv, e_local, h_local,
):
    ny, nxh, nz = geometry
    nx = 2 * nxh
    row = lax.axis_index("row")
    col = lax.axis_index("col")
    y, xh = lax.div(row, nxh), lax.rem(row, nxh)
    z, quad = lax.div(col, 4), lax.rem(col, 4)
    xl, core = lax.div(quad, 2), lax.rem(quad, 2)
    x = xh * 2 + xl
    right, left = lax.rem(z + 1, nz), lax.rem(z + nz - 1, nz)
    right_id = {"col": right * 4 + quad}
    left_id = {"col": left * 4 + quad}
    quad_of = [lax.rem(quad + o, 4) for o in range(1, 4)]
    quad_ids = [{"col": z * 4 + p} for p in quad_of]
    plane_ids = []
    for o in range(1, nx * ny):
        px, py = lax.rem(x + o % nx, nx), lax.rem(y + o // nx, ny)
        plane_ids.append({"row": py * nxh + lax.div(px, 2), "col": z * 4 + lax.rem(px, 2) * 2 + core})
    core_id = {"col": z * 4 + xl * 2 + 1 - core}
    chips = nx * ny
    deep = 16 * max(1, 12 // chips)
    owners, pieces = 192 // deep, 48 // deep
    chip = row * 2 + xl
    active = chip < owners
    own_rows = pl.ds(pl.multiple_of(jnp.where(active, chip, 0) * deep, deep), deep)
    origin = lax.div(jnp.where(active, chip, 0) * deep, 48)
    own_piece = jnp.logical_and(jnp.logical_and(row == z, active), origin == quad)
    home_step = jnp.where(xl == 0, lax.rem(row - z + nz, nz), lax.rem(z - row + nz, nz))
    owner_ids = []
    for m in range(pieces):
        for c in range(2):
            at = quad * pieces + m
            owner_ids.append((
                m, c, jnp.logical_and(own_piece, jnp.logical_and(at == chip, core == c)),
                {"row": lax.div(at, 2), "col": row * 4 + lax.rem(at, 2) * 2 + c},
            ))

    def home_of(s):
        at = jnp.where(origin < 2, z + nz - s, z + s)
        return {"row": z, "col": lax.rem(at, nz) * 4 + origin}

    loads = [
        pltpu.make_async_copy(source, target, load.at[at])
        for at, (source, target) in enumerate(
            [(bias_ref, bias_own), (g_ref, g_own), (o_ref, o_own), (ln_ref, ln_own), (mask_ref, mask_own)]
        )
    ]
    for copy in loads:
        copy.start()

    barrier = pltpu.get_barrier_semaphore()
    greeted = quad_ids + [right_id, left_id] + plane_ids
    for peer in greeted:
        pl.semaphore_signal(barrier, inc=1, device_id=peer, device_id_type=MESH)

    for _, _, same, peer in owner_ids:
        @pl.when(jnp.logical_not(same))
        def _():
            pl.semaphore_signal(barrier, inc=1, device_id=peer, device_id_type=MESH)

    for s in range(nz):
        @pl.when(jnp.logical_and(active, jnp.logical_not(jnp.logical_and(own_piece, s == 0))))
        def _():
            pl.semaphore_signal(barrier, inc=1, device_id=home_of(s), device_id_type=MESH)

    loads[0].wait()
    lanes = jnp.concatenate([bias_own[h] for h in range(HEADS)], axis=1)
    bias_wide[0] = lanes[:, :384]
    bias_wide[1] = lanes[:, 384:]

    for copy in loads[1:]:
        copy.wait()
    lane = iota((48, 128), 1)
    term = lax.rem(lane, 8)
    norm = jnp.concatenate([ln_own[h] for h in range(HEADS)], axis=0) * F32(scaling ** -1)
    norm_terms = [part.astype(BF16) for part in split3(norm)]
    source_lane, target_lane = iota((128, 128), 0), iota((128, 128), 1)
    target_term = lax.rem(target_lane, 8)
    same_head = lax.div(source_lane, 32) == lax.rem(lax.div(target_lane, 8), 4)
    delta_term = jnp.logical_and(target_term >= 3, target_term < 6)
    norm_source, norm_target = iota((64, 128), 0), iota((64, 128), 1)
    norm_row = lax.rem(norm_source, 16)
    norm_fits = jnp.logical_and(
        lax.rem(norm_target, 8) < 3, lax.div(norm_source, 16) == lax.rem(lax.div(norm_target, 8), 4)
    )

    def stats(target, carry):
        total = jnp.zeros((48, 128), F32)
        pick = jnp.where(
            jnp.logical_and(norm_row - target * 4 == lax.div(norm_target, 32), norm_fits), 1.0, 0.0
        ).astype(BF16)
        for part in norm_terms:
            total += lax.dot_general(part, pick, TN, preferred_element_type=F32)
        for i in range(4):
            gather = jnp.where(
                jnp.logical_and(
                    jnp.logical_and(same_head, delta_term), lax.div(target_lane, 32) == i
                ), 1.0, 0.0,
            ).astype(BF16)
            product = g_own[target * 4 + i].astype(F32) * o_own[target * 4 + i].astype(F32)
            high = product.astype(BF16)
            low = (product - high.astype(F32)).astype(BF16)
            total += jnp.dot(high, gather, preferred_element_type=F32)
            total += jnp.dot(low, gather, preferred_element_type=F32)
        high, middle, low = split3(-total)
        value = jnp.where(
            jnp.logical_or(term == 0, term == 3), high,
            jnp.where(jnp.logical_or(term == 1, term == 4), middle,
                      jnp.where(jnp.logical_or(term == 2, term == 5), low,
                                jnp.where(term == 6, 1.0, 0.0))),
        )
        st_out[target] = value.astype(BF16)
        return carry

    lax.fori_loop(0, 4, stats, 0)
    pl.semaphore_wait(barrier,
        len(greeted) + 2 * pieces + jnp.where(active, nz, 0) - jnp.where(own_piece, 2, 0)
    )

    def remote(source, target, send, recv, device):
        return pltpu.make_async_remote_copy(
            src_ref=source, dst_ref=target, send_sem=send, recv_sem=recv,
            device_id=device, device_id_type=MESH,
        )

    place = pl.ds(pl.multiple_of(core * 48, 48), 48)
    mine = pl.ds(pl.multiple_of(quad * 48, 48), 48)

    def swap_row(i, sources):
        kind = 0 if sources is queries_grads else 1
        copies = []
        for at, source in sources:
            target = (qg.at[0, i, xl, at, place, :] if at < 2 else (kx, vx)[at - 2].at[i, mine, :])
            for o in range(3):
                copies.append(remote(
                    source.at[4 * quad_of[o] + i], target,
                    qg_send.at[kind], qg_recv.at[kind, i], quad_ids[o],
                ))
            copies.append(pltpu.make_async_copy(source.at[4 * quad + i], target, qg_local.at[kind, i]))
        return copies

    def swapped(i, kind):
        part = g_own.at[pl.ds(0, 6)]
        remote(part, part, qg_send.at[kind], qg_recv.at[kind, i], core_id).wait_recv()
        part = g_own.at[pl.ds(0, 2)]
        pltpu.make_async_copy(part, part, qg_local.at[kind, i]).wait()

    queries_grads = ((0, q_ref), (1, g_ref))
    keys_values = ((2, k_ref), (3, v_ref))
    for i in range(4):
        for copy in swap_row(i, queries_grads):
            copy.start()

    def push(m, c, peer):
        rows = pl.ds(pl.multiple_of(quad * 48 + m * deep, deep), deep)
        return remote(
            bias_wide.at[c, pl.ds(m * deep, deep)], bias_all.at[home_step, c, rows],
            bp_send.at[m, c], bp_recv.at[home_step], peer,
        )

    for m, c, same, peer in owner_ids:
        @pl.when(jnp.logical_not(same))
        def _():
            push(m, c, peer).start()

        @pl.when(same)
        def _():
            bias_all[0, c, own_rows] = bias_wide[c, m * deep:(m + 1) * deep]

    for i in range(4):
        for copy in swap_row(i, keys_values):
            copy.start()

    def all_of(part, send, recv):
        return remote(part, part, send, recv, core_id)

    def pass_on(s, i):
        return [
            remote(qg.at[s, i, 0], qg.at[s + 1, i, 0], r_send.at[s], r_recv.at[s + 1, i], right_id),
            remote(qg.at[s, i, 1], qg.at[s + 1, i, 1], r_send.at[s], r_recv.at[s + 1, i], left_id),
        ]

    def passed_on(s, i):
        return all_of(qg.at[s + 1, i], r_send.at[s], r_recv.at[s + 1, i])

    def pass_stats(s):
        return [
            remote(st.at[s, 0], st.at[s + 1, 0], s_send.at[s], s_recv.at[s + 1], right_id),
            remote(st.at[s, 1], st.at[s + 1, 1], s_send.at[s], s_recv.at[s + 1], left_id),
        ]

    def passed_stats(s):
        return all_of(st.at[s + 1], s_send.at[s], s_recv.at[s + 1])

    def pass_sum(s, i):
        return [
            remote(acc_out.at[s, i, 0], acc_in.at[s + 1, i, 0], a_send.at[s], a_recv.at[s + 1, i], right_id),
            remote(acc_out.at[s, i, 1], acc_in.at[s + 1, i, 1], a_send.at[s], a_recv.at[s + 1, i], left_id),
        ]

    def passed_sum(s, i):
        return all_of(acc_in.at[s + 1, i], a_send.at[s], a_recv.at[s + 1, i])

    target = st.at[0, xl, place, :]
    stat_swaps = [
        remote(st_out.at[quad_of[o]], target, t_send.at[o], t_recv.at[o], quad_ids[o]) for o in range(3)
    ]
    stat_swaps.append(pltpu.make_async_copy(st_out.at[quad], target, t_local.at[0]))
    for copy in stat_swaps:
        copy.start()

    def clear(s, carry):
        for c in range(2):
            db_acc[s, c] = jnp.zeros((192, 384), F32)
        return carry

    lax.fori_loop(0, nz, clear, 0)

    def start_row(i):
        swapped(i, 0)
        for copy in pass_on(0, i):
            copy.start()

    start_row(0)

    def spread(s):
        @pl.when(active)
        def _():
            part = bias_all.at[s, core, own_rows]

            @pl.when(jnp.logical_not(jnp.logical_and(own_piece, s == 0)))
            def _():
                remote(part, part, bp_send.at[0, 0], bp_recv.at[s], core_id).wait_recv()

            for peer in plane_ids:
                remote(part, part, by_send.at[s], by_recv.at[s], peer).start()

    spread(0)
    start_row(1)
    start_row(2)
    start_row(3)
    for copy in stat_swaps:
        copy.wait()
    for copy in pass_stats(0):
        copy.start()

    wide_lane = iota((192, 128), 1)
    masked = mask_own[:, 0:192]
    for other in range(1, nz):
        masked = jnp.where(z == other, mask_own[:, 192 * other:192 * other + 192], masked)
    masked = jnp.where(masked == 1, 0.0, -BIG).astype(BF16)
    mask_row, mask_lane = iota((16, 128), 0), iota((16, 128), 1)

    def weights(i, carry):
        swapped(i, 1)
        keys, values = kx[i].astype(F32), vx[i].astype(F32)
        pick = jnp.where(
            jnp.logical_and(mask_row == 4 * quad + i, lax.rem(mask_lane, 8) == 6), 1.0, 0.0
        ).astype(BF16)
        mask_lanes = lax.dot_general(masked, pick, TN, preferred_element_type=F32)
        zero = jnp.zeros((192, 128), F32)
        for h in range(HEADS):
            head = lax.div(wide_lane, 32) == h
            block = pl.ds(h * 192, 192)
            offset = wide_lane - (i * 32 + h * 8)
            ws[i, block, 0:128] = jnp.where(head, keys, zero).astype(BF16)
            wp[i, block, 0:128] = jnp.where(head, values, zero).astype(BF16)
            ws[i, block, 128:256] = jnp.where(
                jnp.logical_and(offset >= 0, offset < 3), 1.0, jnp.where(offset == 6, mask_lanes, zero)
            ).astype(BF16)
            wp[i, block, 128:256] = jnp.where(
                jnp.logical_and(offset >= 3, offset < 6), 1.0, zero
            ).astype(BF16)
        ws_t[i] = ws[i].T
        wp_t[i] = wp[i].T
        dk_acc[i] = jnp.zeros(dk_acc.shape[1:], F32)
        dv_acc[i] = jnp.zeros(dv_acc.shape[1:], F32)
        return carry

    def bias_core(s):
        part = bias_all.at[s, core]
        return remote(part, part, bc_send.at[s], bc_recv.at[s], core_id)

    def share_bias(s):
        def gathered(rows):
            part = bias_all.at[s, core, pl.ds(0, rows)]
            remote(part, part, by_send.at[s], by_recv.at[s], core_id).wait_recv()

        pl.when(active)(lambda: gathered(192 - deep))
        pl.when(jnp.logical_not(active))(lambda: gathered(192))
        bias_core(s).start()

    ahead, behind = min(3, nz), min(3, nz)
    for step in range(1, ahead):
        spread(step)
    lax.fori_loop(0, 4, weights, 0)
    for i in range(4):
        passed_on(0, i).wait_recv()
        if nz > 2:
            for copy in pass_on(1, i):
                copy.start()
    share_bias(0)

    def sum_core(s):
        return remote(db_send.at[s], db_core.at[s], dc_send.at[s], dc_recv.at[s], core_id)

    def to_owner(s, c):
        slot = chip - jnp.where(chip > c, 1, 0)
        return remote(
            db_keep.at[s, pl.ds(c * deep, deep)], db_in.at[s, slot], dy_send.at[s], dy_recv.at[s],
            {"row": c // 2, "col": z * 4 + (c % 2) * 2 + core},
        )

    def to_home(s):
        return remote(
            db_part.at[s], db_whole.at[pl.ds(pl.multiple_of(core * 48 + lax.rem(chip * deep, 48), deep), deep)],
            dh_send.at[s], dh_recv.at[0], home_of(s),
        )

    def share_sum(s):
        db_send[s] = db_acc[s, 1 - core].astype(BF16)
        sum_core(s).start()

    def add_cores(s):
        sum_core(s).wait_recv()
        whole = db_acc[s, core] + db_core[s].astype(F32)
        db_acc[s, core] = whole
        db_keep[s] = whole.astype(BF16)
        for c in range(owners):
            @pl.when(c != chip)
            def _():
                to_owner(s, c).start()

    def add_chips(s):
        @pl.when(active)
        def _():
            remote(db_in.at[s], db_in.at[s], dy_send.at[s], dy_recv.at[s], core_id).wait_recv()
            whole = db_acc[s, core, own_rows]
            for o in range(chips - 1):
                whole = whole + db_in[s, o].astype(F32)
            own = jnp.logical_and(own_piece, s == 0)

            @pl.when(own)
            def _():
                db_whole[pl.ds(pl.multiple_of(core * 48 + lax.rem(chip * deep, 48), deep), deep)] = whole.astype(BF16)

            @pl.when(jnp.logical_not(own))
            def _():
                db_part[s] = whole.astype(BF16)
                to_home(s).start()

    def turned(acc, i, factor):
        blocks = []
        for t in range(3):
            unit = jnp.where(iota((64, 128), 0) + 32 * t == iota((64, 128), 1), 1.0, 0.0).astype(BF16)
            part = (acc[i, t] * F32(factor)).astype(BF16)
            blocks.append(lax.dot_general(part, unit, TN, preferred_element_type=F32))
        stacked = jnp.concatenate(blocks, axis=0)
        total = jnp.zeros((192, 128), F32)
        for h in range(HEADS):
            total = jnp.where(lax.div(wide_lane, 32) == h, stacked[192 * h:192 * h + 192], total)
        return total.astype(BF16)

    outs = (dq_out, dk_out, dv_out)

    def give_back(at, i):
        copies = []
        for o in range(3):
            columns = pl.ds(pl.multiple_of(quad_of[o] * 48, 48), 48)
            copies.append(remote(
                back.at[at, i, columns, :], outs[at].at[4 * quad + i],
                e_send.at[at], e_recv.at[at], quad_ids[o],
            ))
        copies.append(pltpu.make_async_copy(back.at[at, i, mine, :], outs[at].at[4 * quad + i], e_local.at[at]))
        return copies

    split = (
        ((0, slice(0, 256)),), ((0, slice(256, 384)), (1, slice(0, 128))), ((1, slice(128, 384)),)
    )

    def two_rows(s, p):
        rows = [2 * p, 2 * p + 1]
        terms = jnp.concatenate([st[s, 0], st[s, 1]], axis=0)
        sides = []
        for i in rows:
            queries = jnp.concatenate([qg[s, i, 0, 0], qg[s, i, 1, 0]], axis=0)
            grads = jnp.concatenate([qg[s, i, 0, 1], qg[s, i, 1, 1]], axis=0)
            sides.append((
                jnp.concatenate([queries, terms], axis=1), jnp.concatenate([grads, terms], axis=1),
                queries.T, grads.T,
            ))
        grad_queries = [jnp.zeros((192, 128), F32) for _ in rows]
        for t in range(3):
            span = pl.ds(256 * t, 256)
            part = slice(32 * t, 32 * t + 64)
            bias = jnp.concatenate([bias_all[s, c, :, lanes] for c, lanes in split[t]], axis=1).astype(F32)
            both = None
            for r, i in enumerate(rows):
                left_s, left_p, queries_t, grads_t = sides[r]
                logits = jnp.dot(left_s, ws_t[i, :, span], preferred_element_type=F32)
                prob_grad = jnp.dot(left_p, wp_t[i, :, span], preferred_element_type=F32)
                probs = jnp.exp(logits * F32(scaling) + bias)
                score_grad = probs * prob_grad
                probs_low = probs.astype(BF16)
                score_low = score_grad.astype(BF16)
                both = score_grad if both is None else both + score_grad
                grad_queries[r] += jnp.dot(score_low, ws[i, span, 0:128], preferred_element_type=F32)
                dk_acc[i, t] += jnp.dot(queries_t[part], score_low, preferred_element_type=F32)
                dv_acc[i, t] += jnp.dot(grads_t[part], probs_low, preferred_element_type=F32)
            begin = 0
            for c, lanes in split[t]:
                width = lanes.stop - lanes.start
                db_acc[s, c, :, lanes] += both[:, begin:begin + width]
                begin += width

        @pl.when(s < nz - 2)
        def _():
            for i in rows:
                passed_on(s + 1, i).wait_recv()

                @pl.when(s < nz - 3)
                def _():
                    for copy in pass_on(s + 2, i):
                        copy.start()

        @pl.when(s == 0)
        def _():
            for i, grad_query in zip(rows, grad_queries):
                dq_own[i] = grad_query

        @pl.when(s == 1)
        def _():
            for i, grad_query in zip(rows, grad_queries):
                acc_out[1, i, 0] = grad_query[:96].astype(BF16)
                acc_out[1, i, 1] = grad_query[96:].astype(BF16)

        @pl.when(s > 1)
        def _():
            for i, grad_query in zip(rows, grad_queries):
                passed_sum(s - 1, i).wait_recv()
                acc_out[s, i, 0] = (grad_query[:96] + acc_in[s, i, 0].astype(F32)).astype(BF16)
                acc_out[s, i, 1] = (grad_query[96:] + acc_in[s, i, 1].astype(F32)).astype(BF16)

        @pl.when(s > 0)
        def _():
            for i in rows:
                for copy in pass_sum(s, i):
                    copy.start()

        @pl.when(s == nz - 1)
        def _():
            for i in rows:
                back[1, i] = turned(dk_acc, i, scaling)
                back[2, i] = turned(dv_acc, i, 1.0)
                for at in (1, 2):
                    for copy in give_back(at, i):
                        copy.start()

    def one_step(s, carry):
        bias_core(s).wait_recv()

        def pair(p, inner):
            two_rows(s, p)

            @pl.when(jnp.logical_and(p == 0, s > 0))
            def _():
                add_cores(s - 1)

            @pl.when(jnp.logical_and(p == 0, s < nz - 1))
            def _():
                share_bias(s + 1)

            @pl.when(jnp.logical_and(p == 0, s < nz - ahead))
            def _():
                spread(s + ahead)

            @pl.when(jnp.logical_and(p == 1, s >= behind))
            def _():
                add_chips(s - behind)

            return inner

        lax.fori_loop(0, 2, pair, 0)
        share_sum(s)

        @pl.when(s < nz - 1)
        def _():
            passed_stats(s).wait_recv()

            @pl.when(s < nz - 2)
            def _():
                for copy in pass_stats(s + 1):
                    copy.start()

        return carry

    lax.fori_loop(0, nz, one_step, 0)

    def finish_query(i, carry):
        passed_sum(nz - 1, i).wait_recv()
        for w in range(2):
            part = pl.ds(96 * w, 96)
            whole = dq_own[i, part, :] + acc_in[nz, i, w].astype(F32)
            back[0, i, part, :] = (whole * F32(scaling)).astype(BF16)
        for copy in give_back(0, i):
            copy.start()
        return carry

    add_cores(nz - 1)
    for step in range(nz - behind, nz - 1):
        add_chips(step)
    lax.fori_loop(0, 4, finish_query, 0)
    add_chips(nz - 1)

    def sent(s, carry):
        @pl.when(s < nz - 1)
        def _():
            all_of(qg.at[s], r_send.at[s], r_recv.at[s, 0]).wait_send()
            passed_stats(s).wait_send()

        @pl.when(s > 0)
        def _():
            all_of(acc_out.at[s], a_send.at[s], a_recv.at[s, 0]).wait_send()

        bias_core(s).wait_send()
        sum_core(s).wait_send()

        @pl.when(active)
        def _():
            remote(db_in.at[s], db_in.at[s], by_send.at[s], by_recv.at[s], core_id).wait_send()
            pl.when(jnp.logical_not(jnp.logical_and(own_piece, s == 0)))(to_home(s).wait_send)

        def passed(rows):
            part = db_keep.at[s, pl.ds(0, rows)]
            remote(part, part, dy_send.at[s], dy_recv.at[s], core_id).wait_send()

        pl.when(active)(lambda: passed(192 - deep))
        pl.when(jnp.logical_not(active))(lambda: passed(192))

        return carry

    lax.fori_loop(0, nz, sent, 0)
    for m, c, same, peer in owner_ids:
        pl.when(jnp.logical_not(same))(push(m, c, peer).wait_send)

    for kind in range(2):
        all_of(g_own.at[pl.ds(0, 12)], qg_send.at[kind], qg_recv.at[kind, 0]).wait_send()
        all_of(g_own.at[pl.ds(0, 12)], qg_send.at[kind], qg_recv.at[kind, 0]).wait_send()
    for at in range(3):
        all_of(back.at[at, pl.ds(0, 3)], e_send.at[at], e_recv.at[at]).wait()
        pltpu.make_async_copy(back.at[at, 0], back.at[at, 0], e_local.at[at]).wait()

    def arrived(rows):
        part = db_whole.at[pl.ds(0, rows)]
        remote(part, part, dh_send.at[0], dh_recv.at[0], core_id).wait_recv()

    pl.when(own_piece)(lambda: arrived(96 - deep))
    pl.when(jnp.logical_not(own_piece))(lambda: arrived(96))
    total = jnp.concatenate([db_whole[0:48], db_whole[48:96]], axis=1).astype(F32)
    for h in range(HEADS):
        db_final[h] = total[:, 192 * h:192 * h + 192].astype(BF16)
    final = pltpu.make_async_copy(db_final, db_out, h_local.at[0])
    final.start()
    final.wait()


def solution(mesh):
    rows_n, cols_n = mesh.shape["row"], mesh.shape["col"]
    nz = cols_n // 4
    nxh = 2 if rows_n >= 4 else 1
    ny = rows_n // nxh
    nx = 2 * nxh
    deep = 16 * max(1, 12 // (nx * ny))

    def shards(query_proj, key_proj, value_proj, attn_out, out_grad, log_norm, pair_mask, pair_bias):
        width = query_proj.shape[2]
        scaling = (width // HEADS) ** -0.5
        anywhere = pl.BlockSpec(memory_space=pl.ANY)
        dma = pltpu.SemaphoreType.DMA
        shapes = (
            jax.ShapeDtypeStruct((16, 48, 128), BF16),
            jax.ShapeDtypeStruct((16, 48, 128), BF16),
            jax.ShapeDtypeStruct((16, 48, 128), BF16),
            jax.ShapeDtypeStruct((HEADS, 48, 192), BF16),
        )
        results = pl.pallas_call(
            functools.partial(kernel, (ny, nxh, nz), scaling),
            out_shape=tuple(pltpu.VMEM(shape.shape, shape.dtype) for shape in shapes),
            in_specs=[anywhere] * 8,
            out_specs=(pl.BlockSpec(memory_space=pltpu.VMEM),) * 4,
            scratch_shapes=[
                pltpu.VMEM((16, 48, 128), BF16),
                pltpu.VMEM((16, 48, 128), BF16),
                pltpu.VMEM((HEADS, 16, 48), F32),
                pltpu.VMEM((16, nz * 192), jnp.int32),
                pltpu.VMEM((HEADS, 48, 192), BF16),
                pltpu.VMEM((2, 48, 384), BF16),
                pltpu.VMEM((nz, 4, 2, 2, 96, 128), BF16),
                pltpu.VMEM((nz, 2, 96, 128), BF16),
                pltpu.VMEM((4, 48, 128), BF16),
                pltpu.VMEM((4, 192, 128), BF16),
                pltpu.VMEM((4, 192, 128), BF16),
                pltpu.VMEM((4, 768, 256), BF16),
                pltpu.VMEM((4, 768, 256), BF16),
                pltpu.VMEM((4, 256, 768), BF16),
                pltpu.VMEM((4, 256, 768), BF16),
                pltpu.VMEM((nz, 2, 192, 384), BF16),
                pltpu.VMEM((nz + 1, 4, 2, 96, 128), BF16),
                pltpu.VMEM((nz, 4, 2, 96, 128), BF16),
                pltpu.VMEM((4, 192, 128), F32),
                pltpu.VMEM((4, 3, 64, 256), F32),
                pltpu.VMEM((4, 3, 64, 256), F32),
                pltpu.VMEM((nz, 2, 192, 384), F32),
                pltpu.VMEM((3, 4, 192, 128), BF16),
                pltpu.VMEM((nz, 192, 384), BF16),
                pltpu.VMEM((nz, 192, 384), BF16),
                pltpu.VMEM((nz, 192, 384), BF16),
                pltpu.VMEM((nz, nx * ny - 1, deep, 384), BF16),
                pltpu.VMEM((nz, deep, 384), BF16),
                pltpu.VMEM((96, 384), BF16),
                pltpu.VMEM((HEADS, 48, 192), BF16),
                dma((5,)),
                dma((2,)), dma((2, 4)), dma((2, 4)),
                dma((3,)), dma((3,)), dma((1,)),
                dma((nz,)), dma((nz, 4)),
                dma((nz,)), dma((nz,)),
                dma((nz,)), dma((nz + 1, 4)),
                dma((48 // deep, 2)), dma((nz,)),
                dma((nz,)), dma((nz,)),
                dma((nz,)), dma((nz,)),
                dma((nz,)), dma((nz,)),
                dma((nz,)), dma((nz,)),
                dma((nz,)), dma((1,)),
                dma((3,)), dma((3,)), dma((3,)),
                dma((1,)),
            ],
            compiler_params=pltpu.CompilerParams(
                collective_id=0, has_side_effects=True, vmem_limit_bytes=56 * 1024 * 1024
            ),
        )(query_proj, key_proj, value_proj, attn_out, out_grad, log_norm, pair_mask, pair_bias)
        return results

    placed = (
        P("row", "col", None), P("row", "col", None), P("row", "col", None), P("row", "col", None),
        P("row", "col", None), P(None, "row", "col"), P("row", None), P(None, "col", "row"),
    )
    return jax.shard_map(
        shards,
        mesh=mesh,
        in_specs=placed,
        out_specs=(P("row", "col", None), P("row", "col", None), P("row", "col", None), P(None, "col", "row")),
        check_vma=False,
    )
```

```python
import functools

import jax
import jax.numpy as jnp
from jax import lax
from jax.experimental import pallas as pl
from jax.experimental.pallas import tpu as pltpu
from jax.sharding import PartitionSpec as P

MESH = pl.DeviceIdType.MESH
HEADS = 4
BIG = 1.0e30
F32 = jnp.float32
BF16 = jnp.bfloat16
NT = (((1,), (1,)), ((), ()))
TN = (((0,), (0,)), ((), ()))


def iota(shape, axis):
    return lax.broadcasted_iota(jnp.int32, shape, axis)


def split3(value):
    high = value.astype(BF16).astype(F32)
    rest = value - high
    middle = rest.astype(BF16).astype(F32)
    low = (rest - middle).astype(BF16).astype(F32)
    return high, middle, low


def kernel(
    geometry, scaling,
    q_ref, k_ref, v_ref, o_ref, g_ref, ln_ref, mask_ref, bias_ref,
    dq_out, dk_out, dv_out, db_out,
    o_own, g_own, ln_own, mask_own, bias_own, bias_wide,
    qg, st, st_in, st_two, st_out, kx, vx, ws, wp, ws_t, wp_t, bias_all,
    acc_in, acc_out, dq_own, dk_acc, dv_acc, db_acc,
    back, db_send, db_core, db_keep, db_in, db_part, db_whole, db_final,
    load, qg_send, qg_recv, qg_local, t_send, t_recv, t_local,
    r_send, r_recv, s_send, s_recv, a_send, a_recv,
    bp_send, bp_recv, by_send, by_recv, bc_send, bc_recv,
    dc_send, dc_recv, dy_send, dy_recv, dh_send, dh_recv,
    e_send, e_recv, e_local, h_local,
):
    ny, nxh, nz = geometry
    nx = 2 * nxh
    row = lax.axis_index("row")
    col = lax.axis_index("col")
    y, xh = lax.div(row, nxh), lax.rem(row, nxh)
    z, quad = lax.div(col, 4), lax.rem(col, 4)
    xl, core = lax.div(quad, 2), lax.rem(quad, 2)
    x = xh * 2 + xl
    right, left = lax.rem(z + 1, nz), lax.rem(z + nz - 1, nz)
    right_id = {"col": right * 4 + quad}
    left_id = {"col": left * 4 + quad}
    quad_of = [lax.rem(quad + o, 4) for o in range(1, 4)]
    quad_ids = [{"col": z * 4 + p} for p in quad_of]
    plane_ids = []
    for o in range(1, nx * ny):
        px, py = lax.rem(x + o % nx, nx), lax.rem(y + o // nx, ny)
        plane_ids.append({"row": py * nxh + lax.div(px, 2), "col": z * 4 + lax.rem(px, 2) * 2 + core})
    core_id = {"col": z * 4 + xl * 2 + 1 - core}
    chips = nx * ny
    deep = 16 * max(1, 12 // chips)
    owners, pieces = 192 // deep, 48 // deep
    chip = row * 2 + xl
    active = chip < owners
    own_rows = pl.ds(pl.multiple_of(jnp.where(active, chip, 0) * deep, deep), deep)
    origin = lax.div(jnp.where(active, chip, 0) * deep, 48)
    own_piece = jnp.logical_and(jnp.logical_and(row == z, active), origin == quad)
    home_step = jnp.where(xl == 0, lax.rem(row - z + nz, nz), lax.rem(z - row + nz, nz))
    owner_ids = []
    for m in range(pieces):
        for c in range(2):
            at = quad * pieces + m
            owner_ids.append((
                m, c, jnp.logical_and(own_piece, jnp.logical_and(at == chip, core == c)),
                {"row": lax.div(at, 2), "col": row * 4 + lax.rem(at, 2) * 2 + c},
            ))

    def home_of(s):
        at = jnp.where(origin < 2, z + nz - s, z + s)
        return {"row": z, "col": lax.rem(at, nz) * 4 + origin}

    loads = [
        pltpu.make_async_copy(source, target, load.at[at])
        for at, (source, target) in enumerate(
            [(bias_ref, bias_own), (g_ref, g_own), (o_ref, o_own), (ln_ref, ln_own), (mask_ref, mask_own)]
        )
    ]
    for copy in loads:
        copy.start()

    barrier = pltpu.get_barrier_semaphore()
    greeted = quad_ids + [right_id, left_id] + plane_ids
    for peer in greeted:
        pl.semaphore_signal(barrier, inc=1, device_id=peer, device_id_type=MESH)

    for _, _, same, peer in owner_ids:
        @pl.when(jnp.logical_not(same))
        def _():
            pl.semaphore_signal(barrier, inc=1, device_id=peer, device_id_type=MESH)

    for s in range(nz):
        @pl.when(jnp.logical_and(active, jnp.logical_not(jnp.logical_and(own_piece, s == 0))))
        def _():
            pl.semaphore_signal(barrier, inc=1, device_id=home_of(s), device_id_type=MESH)

    loads[0].wait()
    lanes = jnp.concatenate([bias_own[h] for h in range(HEADS)], axis=1)
    bias_wide[0] = lanes[:, :384]
    bias_wide[1] = lanes[:, 384:]

    for copy in loads[1:]:
        copy.wait()
    lane = iota((48, 128), 1)
    term = lax.rem(lane, 4)
    norm = jnp.concatenate([ln_own[h] for h in range(HEADS)], axis=0) * F32(scaling ** -1)
    norm_terms = [part.astype(BF16) for part in split3(norm)]
    source_lane, target_lane = iota((128, 128), 0), iota((128, 128), 1)
    same_head = lax.div(source_lane, 32) == lax.rem(lax.div(target_lane, 4), 4)
    delta_term = lax.rem(target_lane, 4) >= 2
    norm_source, norm_target = iota((64, 128), 0), iota((64, 128), 1)
    norm_row = lax.rem(norm_source, 16)
    norm_fits = jnp.logical_and(
        lax.rem(norm_target, 4) < 2, lax.div(norm_source, 16) == lax.rem(lax.div(norm_target, 4), 4)
    )

    def stats(target, carry):
        total = jnp.zeros((48, 128), F32)
        pick = jnp.where(
            jnp.logical_and(norm_row - target * 4 == lax.div(norm_target, 16), norm_fits), 1.0, 0.0
        ).astype(BF16)
        for part in norm_terms:
            total += lax.dot_general(part, pick, TN, preferred_element_type=F32)
        for i in range(4):
            gather = jnp.where(
                jnp.logical_and(
                    jnp.logical_and(same_head, delta_term), lax.div(target_lane, 16) == i
                ), 1.0, 0.0,
            ).astype(BF16)
            product = g_own[target * 4 + i].astype(F32) * o_own[target * 4 + i].astype(F32)
            high = product.astype(BF16)
            low = (product - high.astype(F32)).astype(BF16)
            total += jnp.dot(high, gather, preferred_element_type=F32)
            total += jnp.dot(low, gather, preferred_element_type=F32)
        high, middle, _ = split3(-total)
        value = jnp.where(lax.rem(term, 2) == 0, high, middle)
        value = jnp.where(lane < 64, value, 0.0)
        st_out[target] = value.astype(BF16)
        return carry

    lax.fori_loop(0, 4, stats, 0)
    pl.semaphore_wait(barrier,
        len(greeted) + 2 * pieces + jnp.where(active, nz, 0) - jnp.where(own_piece, 2, 0)
    )

    def remote(source, target, send, recv, device):
        return pltpu.make_async_remote_copy(
            src_ref=source, dst_ref=target, send_sem=send, recv_sem=recv,
            device_id=device, device_id_type=MESH,
        )

    place = pl.ds(pl.multiple_of(core * 48, 48), 48)
    mine = pl.ds(pl.multiple_of(quad * 48, 48), 48)

    def swap_row(i, sources):
        kind = 0 if sources is queries_grads else 1
        copies = []
        for at, source in sources:
            target = (qg.at[0, i, xl, at, place, :] if at < 2 else (kx, vx)[at - 2].at[i, mine, :])
            for o in range(3):
                copies.append(remote(
                    source.at[4 * quad_of[o] + i], target,
                    qg_send.at[kind], qg_recv.at[kind, i], quad_ids[o],
                ))
            copies.append(pltpu.make_async_copy(source.at[4 * quad + i], target, qg_local.at[kind, i]))
        return copies

    def swapped(i, kind):
        part = g_own.at[pl.ds(0, 6)]
        remote(part, part, qg_send.at[kind], qg_recv.at[kind, i], core_id).wait_recv()
        part = g_own.at[pl.ds(0, 2)]
        pltpu.make_async_copy(part, part, qg_local.at[kind, i]).wait()

    queries_grads = ((0, q_ref), (1, g_ref))
    keys_values = ((2, k_ref), (3, v_ref))
    for i in range(4):
        for copy in swap_row(i, queries_grads):
            copy.start()

    def push(m, c, peer):
        rows = pl.ds(pl.multiple_of(quad * 48 + m * deep, deep), deep)
        return remote(
            bias_wide.at[c, pl.ds(m * deep, deep)], bias_all.at[home_step, c, rows],
            bp_send.at[m, c], bp_recv.at[home_step], peer,
        )

    for m, c, same, peer in owner_ids:
        @pl.when(jnp.logical_not(same))
        def _():
            push(m, c, peer).start()

        @pl.when(same)
        def _():
            bias_all[0, c, own_rows] = bias_wide[c, m * deep:(m + 1) * deep]

    for i in range(4):
        for copy in swap_row(i, keys_values):
            copy.start()

    def all_of(part, send, recv):
        return remote(part, part, send, recv, core_id)

    def pass_on(s, i):
        return [
            remote(qg.at[s, i, 0], qg.at[s + 1, i, 0], r_send.at[s], r_recv.at[s + 1, i], right_id),
            remote(qg.at[s, i, 1], qg.at[s + 1, i, 1], r_send.at[s], r_recv.at[s + 1, i], left_id),
        ]

    def passed_on(s, i):
        return all_of(qg.at[s + 1, i], r_send.at[s], r_recv.at[s + 1, i])

    def pass_stats(s):
        return [
            remote(st.at[s, 0], st.at[s + 1, 0], s_send.at[s], s_recv.at[s + 1], right_id),
            remote(st.at[s, 1], st.at[s + 1, 1], s_send.at[s], s_recv.at[s + 1], left_id),
        ]

    def passed_stats(s):
        return all_of(st.at[s + 1], s_send.at[s], s_recv.at[s + 1])

    def pass_sum(s, i):
        return [
            remote(acc_out.at[s, i, 0], acc_in.at[s + 1, i, 0], a_send.at[s], a_recv.at[s + 1, i], right_id),
            remote(acc_out.at[s, i, 1], acc_in.at[s + 1, i, 1], a_send.at[s], a_recv.at[s + 1, i], left_id),
        ]

    def passed_sum(s, i):
        return all_of(acc_in.at[s + 1, i], a_send.at[s], a_recv.at[s + 1, i])

    target = st_in.at[xl, place, :]
    stat_swaps = [
        remote(st_out.at[quad_of[o]], target, t_send.at[o], t_recv.at[o], quad_ids[o]) for o in range(3)
    ]
    stat_swaps.append(pltpu.make_async_copy(st_out.at[quad], target, t_local.at[0]))
    for copy in stat_swaps:
        copy.start()

    def clear(s, carry):
        for c in range(2):
            db_acc[s, c] = jnp.zeros((192, 384), F32)
        return carry

    lax.fori_loop(0, nz, clear, 0)

    def start_row(i):
        swapped(i, 0)
        for copy in pass_on(0, i):
            copy.start()

    start_row(0)

    def spread(s):
        @pl.when(active)
        def _():
            part = bias_all.at[s, core, own_rows]

            @pl.when(jnp.logical_not(jnp.logical_and(own_piece, s == 0)))
            def _():
                remote(part, part, bp_send.at[0, 0], bp_recv.at[s], core_id).wait_recv()

            for peer in plane_ids:
                remote(part, part, by_send.at[s], by_recv.at[s], peer).start()

    spread(0)
    start_row(1)
    start_row(2)
    start_row(3)
    for copy in stat_swaps:
        copy.wait()
    for w in range(2):
        upper = pltpu.roll(st_in[w, 48:96, :].astype(F32), 64, 1)
        st[0, w] = jnp.where(lane < 64, st_in[w, 0:48, :].astype(F32), upper).astype(BF16)
    for copy in pass_stats(0):
        copy.start()

    wide_lane = iota((192, 128), 1)
    masked = mask_own[:, 0:192]
    for other in range(1, nz):
        masked = jnp.where(z == other, mask_own[:, 192 * other:192 * other + 192], masked)
    masked = jnp.where(masked == 1, 0.0, -BIG).astype(BF16)
    mask_row, mask_lane = iota((16, 128), 0), iota((16, 128), 1)

    def weights(i, carry):
        swapped(i, 1)
        keys, values = kx[i].astype(F32), vx[i].astype(F32)
        pick = jnp.where(
            jnp.logical_and(mask_row == 4 * quad + i, mask_lane == 64), 1.0, 0.0
        ).astype(BF16)
        mask_lanes = lax.dot_general(masked, pick, TN, preferred_element_type=F32)
        zero = jnp.zeros((192, 128), F32)
        for h in range(HEADS):
            head = lax.div(wide_lane, 32) == h
            block = pl.ds(h * 192, 192)
            offset = wide_lane - (i * 16 + h * 4)
            ws[i, block, 0:128] = jnp.where(head, keys, zero).astype(BF16)
            wp[i, block, 0:128] = jnp.where(head, values, zero).astype(BF16)
            ws[i, block, 128:256] = jnp.where(
                jnp.logical_and(offset >= 0, offset < 2), 1.0, mask_lanes
            ).astype(BF16)
            wp[i, block, 128:256] = jnp.where(
                jnp.logical_and(offset >= 2, offset < 4), 1.0, zero
            ).astype(BF16)
        ws_t[i] = ws[i].T
        wp_t[i] = wp[i].T
        dk_acc[i] = jnp.zeros(dk_acc.shape[1:], F32)
        dv_acc[i] = jnp.zeros(dv_acc.shape[1:], F32)
        return carry

    def bias_core(s):
        part = bias_all.at[s, core]
        return remote(part, part, bc_send.at[s], bc_recv.at[s], core_id)

    def share_bias(s):
        def gathered(rows):
            part = bias_all.at[s, core, pl.ds(0, rows)]
            remote(part, part, by_send.at[s], by_recv.at[s], core_id).wait_recv()

        pl.when(active)(lambda: gathered(192 - deep))
        pl.when(jnp.logical_not(active))(lambda: gathered(192))
        bias_core(s).start()

    ahead, behind = min(3, nz), min(3, nz)
    for step in range(1, ahead):
        spread(step)
    lax.fori_loop(0, 4, weights, 0)
    for i in range(4):
        passed_on(0, i).wait_recv()
        if nz > 2:
            for copy in pass_on(1, i):
                copy.start()
    share_bias(0)

    def sum_core(s):
        return remote(db_send.at[s], db_core.at[s], dc_send.at[s], dc_recv.at[s], core_id)

    def to_owner(s, c):
        slot = chip - jnp.where(chip > c, 1, 0)
        return remote(
            db_keep.at[s, pl.ds(c * deep, deep)], db_in.at[s, slot], dy_send.at[s], dy_recv.at[s],
            {"row": c // 2, "col": z * 4 + (c % 2) * 2 + core},
        )

    def to_home(s):
        return remote(
            db_part.at[s], db_whole.at[pl.ds(pl.multiple_of(core * 48 + lax.rem(chip * deep, 48), deep), deep)],
            dh_send.at[s], dh_recv.at[0], home_of(s),
        )

    def share_sum(s):
        db_send[s] = db_acc[s, 1 - core].astype(BF16)
        sum_core(s).start()

    def add_cores(s):
        sum_core(s).wait_recv()
        whole = db_acc[s, core] + db_core[s].astype(F32)
        db_acc[s, core] = whole
        db_keep[s] = whole.astype(BF16)
        for c in range(owners):
            @pl.when(c != chip)
            def _():
                to_owner(s, c).start()

    def add_chips(s):
        @pl.when(active)
        def _():
            remote(db_in.at[s], db_in.at[s], dy_send.at[s], dy_recv.at[s], core_id).wait_recv()
            whole = db_acc[s, core, own_rows]
            for o in range(chips - 1):
                whole = whole + db_in[s, o].astype(F32)
            own = jnp.logical_and(own_piece, s == 0)

            @pl.when(own)
            def _():
                db_whole[pl.ds(pl.multiple_of(core * 48 + lax.rem(chip * deep, 48), deep), deep)] = whole.astype(BF16)

            @pl.when(jnp.logical_not(own))
            def _():
                db_part[s] = whole.astype(BF16)
                to_home(s).start()

    def turned(acc, i, factor):
        blocks = []
        for t in range(3):
            unit = jnp.where(iota((64, 128), 0) + 32 * t == iota((64, 128), 1), 1.0, 0.0).astype(BF16)
            part = (acc[i, t] * F32(factor)).astype(BF16)
            blocks.append(lax.dot_general(part, unit, TN, preferred_element_type=F32))
        stacked = jnp.concatenate(blocks, axis=0)
        total = jnp.zeros((192, 128), F32)
        for h in range(HEADS):
            total = jnp.where(lax.div(wide_lane, 32) == h, stacked[192 * h:192 * h + 192], total)
        return total.astype(BF16)

    outs = (dq_out, dk_out, dv_out)

    def give_back(at, i):
        copies = []
        for o in range(3):
            columns = pl.ds(pl.multiple_of(quad_of[o] * 48, 48), 48)
            copies.append(remote(
                back.at[at, i, columns, :], outs[at].at[4 * quad + i],
                e_send.at[at], e_recv.at[at], quad_ids[o],
            ))
        copies.append(pltpu.make_async_copy(back.at[at, i, mine, :], outs[at].at[4 * quad + i], e_local.at[at]))
        return copies

    split = (
        ((0, slice(0, 256)),), ((0, slice(256, 384)), (1, slice(0, 128))), ((1, slice(128, 384)),)
    )

    def two_rows(s, p):
        rows = [2 * p, 2 * p + 1]
        terms = st_two[...]
        sides = []
        for i in rows:
            queries = jnp.concatenate([qg[s, i, 0, 0], qg[s, i, 1, 0]], axis=0)
            grads = jnp.concatenate([qg[s, i, 0, 1], qg[s, i, 1, 1]], axis=0)
            sides.append((
                jnp.concatenate([queries, terms], axis=1), jnp.concatenate([grads, terms], axis=1),
                queries.T, grads.T,
            ))
        grad_queries = [jnp.zeros((192, 128), F32) for _ in rows]
        for t in range(3):
            span = pl.ds(256 * t, 256)
            part = slice(32 * t, 32 * t + 64)
            bias = jnp.concatenate([bias_all[s, c, :, lanes] for c, lanes in split[t]], axis=1).astype(F32)
            both = None
            for r, i in enumerate(rows):
                left_s, left_p, queries_t, grads_t = sides[r]
                logits = jnp.dot(left_s, ws_t[i, :, span], preferred_element_type=F32)
                prob_grad = jnp.dot(left_p, wp_t[i, :, span], preferred_element_type=F32)
                probs = jnp.exp(logits * F32(scaling) + bias)
                score_grad = probs * prob_grad
                probs_low = probs.astype(BF16)
                score_low = score_grad.astype(BF16)
                both = score_grad if both is None else both + score_grad
                grad_queries[r] += jnp.dot(score_low, ws[i, span, 0:128], preferred_element_type=F32)
                dk_acc[i, t] += jnp.dot(queries_t[part], score_low, preferred_element_type=F32)
                dv_acc[i, t] += jnp.dot(grads_t[part], probs_low, preferred_element_type=F32)
            begin = 0
            for c, lanes in split[t]:
                width = lanes.stop - lanes.start
                db_acc[s, c, :, lanes] += both[:, begin:begin + width]
                begin += width

        @pl.when(s < nz - 2)
        def _():
            for i in rows:
                passed_on(s + 1, i).wait_recv()

                @pl.when(s < nz - 3)
                def _():
                    for copy in pass_on(s + 2, i):
                        copy.start()

        @pl.when(s == 0)
        def _():
            for i, grad_query in zip(rows, grad_queries):
                dq_own[i] = grad_query

        @pl.when(s == 1)
        def _():
            for i, grad_query in zip(rows, grad_queries):
                acc_out[1, i, 0] = grad_query[:96].astype(BF16)
                acc_out[1, i, 1] = grad_query[96:].astype(BF16)

        @pl.when(s > 1)
        def _():
            for i, grad_query in zip(rows, grad_queries):
                passed_sum(s - 1, i).wait_recv()
                acc_out[s, i, 0] = (grad_query[:96] + acc_in[s, i, 0].astype(F32)).astype(BF16)
                acc_out[s, i, 1] = (grad_query[96:] + acc_in[s, i, 1].astype(F32)).astype(BF16)

        @pl.when(s > 0)
        def _():
            for i in rows:
                for copy in pass_sum(s, i):
                    copy.start()

        @pl.when(s == nz - 1)
        def _():
            for i in rows:
                back[1, i] = turned(dk_acc, i, scaling)
                back[2, i] = turned(dv_acc, i, 1.0)
                for at in (1, 2):
                    for copy in give_back(at, i):
                        copy.start()

    def one_step(s, carry):
        for w in range(2):
            packed = st[s, w].astype(F32)
            for c, part in enumerate((packed, pltpu.roll(packed, 64, 1))):
                part = jnp.where(lane < 64, part, jnp.where(lane == 64, 1.0, 0.0))
                st_two[96 * w + 48 * c:96 * w + 48 * c + 48, :] = part.astype(BF16)

        bias_core(s).wait_recv()

        def pair(p, inner):
            two_rows(s, p)

            @pl.when(jnp.logical_and(p == 0, s > 0))
            def _():
                add_cores(s - 1)

            @pl.when(jnp.logical_and(p == 0, s < nz - 1))
            def _():
                share_bias(s + 1)

            @pl.when(jnp.logical_and(p == 0, s < nz - ahead))
            def _():
                spread(s + ahead)

            @pl.when(jnp.logical_and(p == 1, s >= behind))
            def _():
                add_chips(s - behind)

            return inner

        lax.fori_loop(0, 2, pair, 0)
        share_sum(s)

        @pl.when(s < nz - 1)
        def _():
            passed_stats(s).wait_recv()

            @pl.when(s < nz - 2)
            def _():
                for copy in pass_stats(s + 1):
                    copy.start()

        return carry

    lax.fori_loop(0, nz, one_step, 0)

    def finish_query(i, carry):
        passed_sum(nz - 1, i).wait_recv()
        for w in range(2):
            part = pl.ds(96 * w, 96)
            whole = dq_own[i, part, :] + acc_in[nz, i, w].astype(F32)
            back[0, i, part, :] = (whole * F32(scaling)).astype(BF16)
        for copy in give_back(0, i):
            copy.start()
        return carry

    add_cores(nz - 1)
    for step in range(nz - behind, nz - 1):
        add_chips(step)
    lax.fori_loop(0, 4, finish_query, 0)
    add_chips(nz - 1)

    def sent(s, carry):
        @pl.when(s < nz - 1)
        def _():
            all_of(qg.at[s], r_send.at[s], r_recv.at[s, 0]).wait_send()
            passed_stats(s).wait_send()

        @pl.when(s > 0)
        def _():
            all_of(acc_out.at[s], a_send.at[s], a_recv.at[s, 0]).wait_send()

        bias_core(s).wait_send()
        sum_core(s).wait_send()

        @pl.when(active)
        def _():
            remote(db_in.at[s], db_in.at[s], by_send.at[s], by_recv.at[s], core_id).wait_send()
            pl.when(jnp.logical_not(jnp.logical_and(own_piece, s == 0)))(to_home(s).wait_send)

        def passed(rows):
            part = db_keep.at[s, pl.ds(0, rows)]
            remote(part, part, dy_send.at[s], dy_recv.at[s], core_id).wait_send()

        pl.when(active)(lambda: passed(192 - deep))
        pl.when(jnp.logical_not(active))(lambda: passed(192))

        return carry

    lax.fori_loop(0, nz, sent, 0)
    for m, c, same, peer in owner_ids:
        pl.when(jnp.logical_not(same))(push(m, c, peer).wait_send)

    for kind in range(2):
        all_of(g_own.at[pl.ds(0, 12)], qg_send.at[kind], qg_recv.at[kind, 0]).wait_send()
        all_of(g_own.at[pl.ds(0, 12)], qg_send.at[kind], qg_recv.at[kind, 0]).wait_send()
    for at in range(3):
        all_of(back.at[at, pl.ds(0, 3)], e_send.at[at], e_recv.at[at]).wait()
        pltpu.make_async_copy(back.at[at, 0], back.at[at, 0], e_local.at[at]).wait()

    def arrived(rows):
        part = db_whole.at[pl.ds(0, rows)]
        remote(part, part, dh_send.at[0], dh_recv.at[0], core_id).wait_recv()

    pl.when(own_piece)(lambda: arrived(96 - deep))
    pl.when(jnp.logical_not(own_piece))(lambda: arrived(96))
    total = jnp.concatenate([db_whole[0:48], db_whole[48:96]], axis=1).astype(F32)
    for h in range(HEADS):
        db_final[h] = total[:, 192 * h:192 * h + 192].astype(BF16)
    final = pltpu.make_async_copy(db_final, db_out, h_local.at[0])
    final.start()
    final.wait()


def solution(mesh):
    rows_n, cols_n = mesh.shape["row"], mesh.shape["col"]
    nz = cols_n // 4
    nxh = 2 if rows_n >= 4 else 1
    ny = rows_n // nxh
    nx = 2 * nxh
    deep = 16 * max(1, 12 // (nx * ny))

    def shards(query_proj, key_proj, value_proj, attn_out, out_grad, log_norm, pair_mask, pair_bias):
        width = query_proj.shape[2]
        scaling = (width // HEADS) ** -0.5
        anywhere = pl.BlockSpec(memory_space=pl.ANY)
        dma = pltpu.SemaphoreType.DMA
        shapes = (
            jax.ShapeDtypeStruct((16, 48, 128), BF16),
            jax.ShapeDtypeStruct((16, 48, 128), BF16),
            jax.ShapeDtypeStruct((16, 48, 128), BF16),
            jax.ShapeDtypeStruct((HEADS, 48, 192), BF16),
        )
        results = pl.pallas_call(
            functools.partial(kernel, (ny, nxh, nz), scaling),
            out_shape=tuple(pltpu.VMEM(shape.shape, shape.dtype) for shape in shapes),
            in_specs=[anywhere] * 8,
            out_specs=(pl.BlockSpec(memory_space=pltpu.VMEM),) * 4,
            scratch_shapes=[
                pltpu.VMEM((16, 48, 128), BF16),
                pltpu.VMEM((16, 48, 128), BF16),
                pltpu.VMEM((HEADS, 16, 48), F32),
                pltpu.VMEM((16, nz * 192), jnp.int32),
                pltpu.VMEM((HEADS, 48, 192), BF16),
                pltpu.VMEM((2, 48, 384), BF16),
                pltpu.VMEM((nz, 4, 2, 2, 96, 128), BF16),
                pltpu.VMEM((nz, 2, 48, 128), BF16),
                pltpu.VMEM((2, 96, 128), BF16),
                pltpu.VMEM((192, 128), BF16),
                pltpu.VMEM((4, 48, 128), BF16),
                pltpu.VMEM((4, 192, 128), BF16),
                pltpu.VMEM((4, 192, 128), BF16),
                pltpu.VMEM((4, 768, 256), BF16),
                pltpu.VMEM((4, 768, 256), BF16),
                pltpu.VMEM((4, 256, 768), BF16),
                pltpu.VMEM((4, 256, 768), BF16),
                pltpu.VMEM((nz, 2, 192, 384), BF16),
                pltpu.VMEM((nz + 1, 4, 2, 96, 128), BF16),
                pltpu.VMEM((nz, 4, 2, 96, 128), BF16),
                pltpu.VMEM((4, 192, 128), F32),
                pltpu.VMEM((4, 3, 64, 256), F32),
                pltpu.VMEM((4, 3, 64, 256), F32),
                pltpu.VMEM((nz, 2, 192, 384), F32),
                pltpu.VMEM((3, 4, 192, 128), BF16),
                pltpu.VMEM((nz, 192, 384), BF16),
                pltpu.VMEM((nz, 192, 384), BF16),
                pltpu.VMEM((nz, 192, 384), BF16),
                pltpu.VMEM((nz, nx * ny - 1, deep, 384), BF16),
                pltpu.VMEM((nz, deep, 384), BF16),
                pltpu.VMEM((96, 384), BF16),
                pltpu.VMEM((HEADS, 48, 192), BF16),
                dma((5,)),
                dma((2,)), dma((2, 4)), dma((2, 4)),
                dma((3,)), dma((3,)), dma((1,)),
                dma((nz,)), dma((nz, 4)),
                dma((nz,)), dma((nz,)),
                dma((nz,)), dma((nz + 1, 4)),
                dma((48 // deep, 2)), dma((nz,)),
                dma((nz,)), dma((nz,)),
                dma((nz,)), dma((nz,)),
                dma((nz,)), dma((nz,)),
                dma((nz,)), dma((nz,)),
                dma((nz,)), dma((1,)),
                dma((3,)), dma((3,)), dma((3,)),
                dma((1,)),
            ],
            compiler_params=pltpu.CompilerParams(
                collective_id=0, has_side_effects=True, vmem_limit_bytes=56 * 1024 * 1024
            ),
        )(query_proj, key_proj, value_proj, attn_out, out_grad, log_norm, pair_mask, pair_bias)
        return results

    placed = (
        P("row", "col", None), P("row", "col", None), P("row", "col", None), P("row", "col", None),
        P("row", "col", None), P(None, "row", "col"), P("row", None), P(None, "col", "row"),
    )
    return jax.shard_map(
        shards,
        mesh=mesh,
        in_specs=placed,
        out_specs=(P("row", "col", None), P("row", "col", None), P("row", "col", None), P(None, "col", "row")),
        check_vma=False,
    )
```
